512 devices in a mesh: rows: 32 (over z, core), tp: 4 (over x), attn: 4 (over y).
Axes of the slice: x: 4, y: 4, z: 16, core: 2. Of those that a mesh axis runs over, the one named last changes fastest.
Arguments:
- tokens: bfloat16 [65536, 4096], P(('rows', 'attn')), may hold values from -60 to 60, as said below
- norm_gain: bfloat16 [4096], replicated, may hold values from 0.099609375 to 1.8984375
- w_query: bfloat16 [4096, 2048], P('rows', 'tp'), may hold values from -1 to 1, as said below
- key_projection_weight: bfloat16 [4096, 512], P('rows', 'tp'), may hold values from -8 to 8, as said below
- value_projection_weight: bfloat16 [4096, 512], P('rows', 'tp'), may hold values from -0.09375 to 0.09375
- documents: int32 [32, 2048], P('rows'), may hold values from 0 to 5, never falling along the last dimension, each value on 1 to 1024 neighbouring positions
Outputs:
- attn_out: bfloat16 [65536, 2048], P(('rows', 'attn'), 'tp')
The draws below stay inside these ranges and needn't reach their ends.
Inputs may be any that keep to these rules, and one draw needn't show every extreme that they name: `tokens`: activations of order one. `w_query`: entries of order 4096 ** -0.5. `key_projection_weight`: entries of order one or smaller. `documents`: along each window the document numbers never fall; every document spans 1 to 1024 tokens and some document of each window spans exactly 1024.
All inputs are finite; a program needn't handle non-finite values.
Results may differ from the reference program's by a relative error of at most 0.012.
The reference program's roundings to bfloat16 on the way count: a program that leaves them out, or rounds other values in their place, can miss the bound.
Values may be sent and summed in bfloat16 or wider, within the bound.
No kernel may reach another device: no remote copies, remote signals or barrier semaphores. Data moves between devices by JAX's collectives and lax.ppermute only.
A program may use at most 64 MiB of HBM per device.

```python
import math
import jax
import jax.numpy as jnp
import numpy as np
from jax import lax

MODEL_WIDTH = 4096
QUERY_HEADS = 16
KEY_VALUE_HEADS = 4
HEAD_SIZE = 128
DOCS = 6
WINDOW_TOKENS = 2048
MOST = 1024
TOKENS = 65536
N_ROWS = 32


def draw_tokens(key, part):
    base = jax.random.normal(jax.random.fold_in(key, 11), (TOKENS, MODEL_WIDTH), jnp.float32)
    row_scale = jnp.exp(jax.random.uniform(jax.random.fold_in(key, 12), (TOKENS, 1), jnp.float32, math.log(0.3), math.log(3.0)))
    column_scale = jnp.exp(jax.random.uniform(jax.random.fold_in(key, 13), (1, MODEL_WIDTH), jnp.float32, math.log(0.3), math.log(3.0)))
    return jnp.clip(base * row_scale * column_scale, -60.0, 60.0).astype(jnp.bfloat16)


def projection_pair(key):
    query_matrix = jax.random.normal(jax.random.fold_in(key, 21), (MODEL_WIDTH, QUERY_HEADS * HEAD_SIZE), jnp.float32) * MODEL_WIDTH ** (-0.5)
    key_matrix = jax.random.normal(jax.random.fold_in(key, 22), (MODEL_WIDTH, KEY_VALUE_HEADS * HEAD_SIZE), jnp.float32) * MODEL_WIDTH ** (-0.5)
    return (jnp.clip(query_matrix, -1.0, 1.0), jnp.clip(key_matrix, -8.0, 8.0))


def draw_w_query(key, part):
    return projection_pair(key)[0].astype(jnp.bfloat16)


def draw_key_projection_weight(key, part):
    return projection_pair(key)[1].astype(jnp.bfloat16)


def block_scale(stream_key, extent, shards, smallest, high):
    level = 1.0
    for axis_at, blocks in shards:
        draws = jax.random.uniform(jax.random.fold_in(jax.random.fold_in(stream_key, 6), axis_at), (blocks,), jnp.float32, smallest / len(shards), high / len(shards))
        level = level * jnp.repeat(jnp.exp(draws), extent[axis_at] // blocks).reshape((-1,) + (1,) * (len(extent) - 1 - axis_at))
    return level


def length_profile(amount, total, limit, skew):
    loads = [(1 << 20) // math.isqrt(standing ** skew) + 1 for standing in range(2, amount + 1)]
    spare, given = total - limit - (amount - 1), [1] * (amount - 1)
    while spare > 0:
        movable = [i for i in range(amount - 1) if given[i] < limit]
        mass, left = sum([loads[i] for i in movable]), spare
        for i in movable:
            more = min(limit - given[i], max(1, left * loads[i] // mass), spare)
            given[i] = given[i] + more
            spare = spare - more
    return np.array([limit] + given)


def ragged_sizes(stream_key, count, total, most, lean):
    if count == 2:
        one = jax.random.randint(stream_key, (), max(1, total - most), min(most, total - 1) + 1)
        return jnp.stack([one, total - one])
    lengths = jnp.asarray(length_profile(count, total, most, lean), jnp.int32)
    pairs = (count - 1) // 2
    source_of, receiver = lengths[1:1 + 2 * pairs:2], lengths[2:2 + 2 * pairs:2]
    margin = jnp.minimum(source_of - 1, most - receiver)
    shifted = jax.random.randint(jax.random.fold_in(stream_key, 1), (pairs,), 0, 1 << 20) % (margin + 1)
    lengths = lengths.at[1:1 + 2 * pairs:2].set(source_of - shifted).at[2:2 + 2 * pairs:2].set(receiver + shifted)
    return lengths[jax.random.permutation(jax.random.fold_in(stream_key, 2), count)]


def gaussian(own_key, shape, scale, limit, pieces=(), kind=jnp.bfloat16):
    result = jax.random.normal(own_key, shape, jnp.float32) * scale
    if len(pieces) > 0:
        result = block_scale(own_key, shape, pieces, -0.22, 0.18) * result
    return jnp.clip(result, min=-limit, max=limit).astype(kind)


def setup_inputs(seed: int = 0) -> dict:
    streams_of = jax.random.split(jax.random.key(seed), 7)
    tokens = draw_tokens(jax.random.fold_in(streams_of[6], 71), 0)
    norm_gain = jnp.clip(1.0 + 0.18 * jax.random.normal(streams_of[1], (MODEL_WIDTH,), jnp.float32), 0.099609375, 1.8984375).astype(jnp.bfloat16)
    w_query = draw_w_query(jax.random.fold_in(streams_of[6], 71), 0)
    key_projection_weight = draw_key_projection_weight(jax.random.fold_in(streams_of[6], 71), 0)
    value_projection_weight = gaussian(streams_of[4], (MODEL_WIDTH, KEY_VALUE_HEADS * HEAD_SIZE), MODEL_WIDTH ** -0.5, 0.09375, ((0, 32), (1, 4)))
    documents = jax.vmap(lambda own: jnp.searchsorted(jnp.cumsum(ragged_sizes(own, DOCS, WINDOW_TOKENS, MOST, 2)), jnp.arange(WINDOW_TOKENS), side="right"))(jax.random.split(streams_of[5], N_ROWS)).reshape((N_ROWS, WINDOW_TOKENS)).astype(jnp.int32)
    return {"tokens": tokens, "norm_gain": norm_gain, "w_query": w_query, "key_projection_weight": key_projection_weight, "value_projection_weight": value_projection_weight, "documents": documents}


def rotary(vectors, positions):
    head_dim = vectors.shape[-1]
    half_dim = head_dim // 2
    frequency = jnp.exp(jnp.arange(half_dim, dtype=jnp.float32) * (-2.0 * math.log(500000.0) / head_dim))
    angles = positions.astype(jnp.float32)[:, None] * frequency[None, :]
    cosine_table = jnp.cos(angles)[:, None, :]
    sine_table = jnp.sin(angles)[:, None, :]
    first_half = vectors[..., :half_dim]
    second_half = vectors[..., half_dim:]
    return jnp.concatenate([first_half * cosine_table - second_half * sine_table, second_half * cosine_table + first_half * sine_table], axis=-1)

def rms_normed(tokens, norm_gain):
    widened = tokens.astype(jnp.float32)
    mean_sq = lax.optimization_barrier(jnp.mean(widened * widened, axis=-1, keepdims=True))
    return (widened * lax.rsqrt(mean_sq + 1e-05) * norm_gain.astype(jnp.float32)).astype(jnp.bfloat16)

def reference(tokens, norm_gain, w_query, key_projection_weight, value_projection_weight, documents):
    group_width = QUERY_HEADS // KEY_VALUE_HEADS
    score_scale = 1.0 / math.sqrt(HEAD_SIZE)
    windows = tokens.reshape(N_ROWS, WINDOW_TOKENS, MODEL_WIDTH)

    def one_window(inputs):
        window, doc_ids = inputs
        normalized_input = rms_normed(window, norm_gain)
        positions = jnp.arange(WINDOW_TOKENS, dtype=jnp.int32)
        query_proj = jnp.dot(normalized_input, w_query, preferred_element_type=jnp.float32).reshape(WINDOW_TOKENS, QUERY_HEADS, HEAD_SIZE)
        key_projected = jnp.dot(normalized_input, key_projection_weight, preferred_element_type=jnp.float32).reshape(WINDOW_TOKENS, KEY_VALUE_HEADS, HEAD_SIZE)
        query_vectors_all = rotary(query_proj, positions).astype(jnp.bfloat16)
        keys_all = rotary(key_projected, positions).astype(jnp.bfloat16)
        value_vectors_all = jnp.dot(normalized_input, value_projection_weight, preferred_element_type=jnp.float32).astype(jnp.bfloat16).reshape(WINDOW_TOKENS, KEY_VALUE_HEADS, HEAD_SIZE)
        visible = (doc_ids[:, None] == doc_ids[None, :]) & (positions[:, None] >= positions[None, :])
        grouped_heads = query_vectors_all.reshape(WINDOW_TOKENS, KEY_VALUE_HEADS, group_width, HEAD_SIZE)

        def single_head(head_index):
            query_head = lax.dynamic_index_in_dim(grouped_heads, head_index, 1, keepdims=False)
            key_head = lax.dynamic_index_in_dim(keys_all, head_index, 1, keepdims=False)
            value_head = lax.dynamic_index_in_dim(value_vectors_all, head_index, 1, keepdims=False)
            scores = jnp.einsum('pgd,jd->gpj', query_head.astype(jnp.float32), key_head.astype(jnp.float32)) * score_scale
            scores = jnp.where(visible[None], scores, -1e+30)
            row_max = lax.optimization_barrier(jnp.max(scores, axis=-1, keepdims=True))
            weights = jnp.where(visible[None], jnp.exp(scores - row_max), 0.0)
            row_total = lax.optimization_barrier(jnp.sum(weights, axis=-1))
            rounded = weights.astype(jnp.bfloat16)
            mixed_out = jnp.einsum('gpj,jd->gpd', rounded.astype(jnp.float32), value_head.astype(jnp.float32))
            return mixed_out / row_total[..., None]
        split_by_head = lax.map(single_head, jnp.arange(KEY_VALUE_HEADS, dtype=jnp.int32))
        return jnp.transpose(split_by_head, (2, 0, 1, 3)).reshape(WINDOW_TOKENS, QUERY_HEADS * HEAD_SIZE).astype(jnp.bfloat16)
    outputs = lax.map(one_window, (windows, documents))
    return outputs.reshape(N_ROWS * WINDOW_TOKENS, QUERY_HEADS * HEAD_SIZE)
```

```python
import functools
import math

import jax
import jax.numpy as jnp
from jax import lax
from jax.experimental import pallas as pl
from jax.experimental.pallas import tpu as pltpu
from jax.sharding import PartitionSpec as P

HEAD_SIZE = 128
KEY_BLOCK = 256
QUERY_BLOCK = 128


def rotary_tables(positions):
    half_dim = HEAD_SIZE // 2
    frequency = jnp.exp(
        jnp.arange(half_dim, dtype=jnp.float32) * (-2.0 * math.log(500000.0) / HEAD_SIZE)
    )
    angles = positions.astype(jnp.float32)[:, None] * frequency[None, :]
    cosine, sine = jnp.cos(angles), jnp.sin(angles)
    return jnp.concatenate([cosine, cosine], 1), jnp.concatenate([-sine, sine], 1)


def project_kernel(rotated_heads, x_ref, w_ref, cos_ref, sin_ref, out_ref, acc_ref):
    step = pl.program_id(0)
    part = jnp.dot(x_ref[...], w_ref[...], preferred_element_type=jnp.float32)

    @pl.when(step == 0)
    def _():
        acc_ref[...] = part

    @pl.when(step > 0)
    def _():
        acc_ref[...] += part

    @pl.when(step == pl.num_programs(0) - 1)
    def _():
        for head in range(out_ref.shape[1] // HEAD_SIZE):
            lanes = slice(head * HEAD_SIZE, (head + 1) * HEAD_SIZE)
            u = acc_ref[:, lanes]
            if head < rotated_heads:
                u = u * cos_ref[...] + pltpu.roll(u, HEAD_SIZE // 2, 1) * sin_ref[...]
            out_ref[:, lanes] = u.astype(jnp.bfloat16)


def project(x, w, cosine, sine, rotated_heads, steps=4):
    rows, depth = x.shape
    width = w.shape[1]
    chunk = depth // steps
    return pl.pallas_call(
        functools.partial(project_kernel, rotated_heads),
        grid=(steps,),
        in_specs=[
            pl.BlockSpec((rows, chunk), lambda s: (0, s)),
            pl.BlockSpec((chunk, width), lambda s: (s, 0)),
            pl.BlockSpec((rows, HEAD_SIZE), lambda s: (0, 0)),
            pl.BlockSpec((rows, HEAD_SIZE), lambda s: (0, 0)),
        ],
        out_specs=pl.BlockSpec((rows, width), lambda s: (0, 0)),
        out_shape=jax.ShapeDtypeStruct((rows, width), jnp.bfloat16),
        scratch_shapes=[pltpu.VMEM((rows, width), jnp.float32)],
        compiler_params=pltpu.CompilerParams(vmem_limit_bytes=32 * 1024 * 1024),
        cost_estimate=pl.CostEstimate(
            flops=2 * rows * depth * width,
            bytes_accessed=2 * (rows * depth + depth * width + rows * width),
            transcendentals=0,
        ),
    )(x, w, cosine, sine)


def attend_kernel(first_ref, q_ref, low_ref, kv2_ref, kv1_ref, kv0_ref, out_ref, kv, sems):
    step = pl.program_id(0)
    rows = kv0_ref.shape[0]
    sources = (kv2_ref, kv1_ref, kv0_ref)

    @pl.when(step == 0)
    def _():
        copies = [
            pltpu.make_async_copy(src, kv.at[pl.ds(n * rows, rows)], sems.at[n])
            for n, src in enumerate(sources)
        ]
        for copy in copies:
            copy.start()
        for copy in copies:
            copy.wait()

    heads = q_ref.shape[1] // HEAD_SIZE
    block = q_ref.shape[0]
    q = jnp.concatenate(
        [q_ref[:, h * HEAD_SIZE : (h + 1) * HEAD_SIZE] for h in range(heads)], axis=0
    )
    low = low_ref[...]
    first_query = 2 * rows + step * block
    query_at = first_query + lax.broadcasted_iota(jnp.int32, (block, KEY_BLOCK), 0)
    lane = lax.broadcasted_iota(jnp.int32, (block, KEY_BLOCK), 1)
    to_log2 = math.log2(math.e) / math.sqrt(HEAD_SIZE)

    def visit(n, carry):
        run_max, run_sum, run_acc = carry
        start = pl.multiple_of(n * KEY_BLOCK, KEY_BLOCK)
        keys = kv[pl.ds(start, KEY_BLOCK), :HEAD_SIZE]
        values = kv[pl.ds(start, KEY_BLOCK), HEAD_SIZE:]
        scores = lax.dot_general(
            q, keys, (((1,), (1,)), ((), ())), preferred_element_type=jnp.float32
        )
        key_at = start + lane
        visible = (key_at >= low) & (key_at <= query_at)
        scores = jnp.where(visible[None], scores.reshape(heads, block, KEY_BLOCK), -1e30)
        scores = scores.reshape(heads * block, KEY_BLOCK)
        new_max = jnp.maximum(run_max, jnp.max(scores, axis=-1, keepdims=True))
        factor = jnp.exp2((run_max - new_max) * to_log2)
        weights = jnp.exp2((scores - new_max) * to_log2)
        run_sum = run_sum * factor + jnp.sum(weights, axis=-1, keepdims=True)
        run_acc = run_acc * factor + jnp.dot(
            weights.astype(jnp.bfloat16), values, preferred_element_type=jnp.float32
        )
        return new_max, run_sum, run_acc

    initial = (
        jnp.full((heads * block, 1), -1e30, jnp.float32),
        jnp.zeros((heads * block, 1), jnp.float32),
        jnp.zeros((heads * block, HEAD_SIZE), jnp.float32),
    )
    last = (first_query + block - 1) // KEY_BLOCK + 1
    _, run_sum, run_acc = lax.fori_loop(first_ref[step], last, visit, initial)
    mixed = (run_acc / run_sum).astype(jnp.bfloat16)
    for h in range(heads):
        out_ref[:, h * HEAD_SIZE : (h + 1) * HEAD_SIZE] = mixed[h * block : (h + 1) * block]


def attend(q, low, kv2, kv1, kv0):
    rows, width = q.shape
    first = low[:: QUERY_BLOCK, 0] // KEY_BLOCK
    spec = pltpu.PrefetchScalarGridSpec(
        num_scalar_prefetch=1,
        grid=(rows // QUERY_BLOCK,),
        in_specs=[
            pl.BlockSpec((QUERY_BLOCK, width), lambda s, first: (s, 0)),
            pl.BlockSpec((QUERY_BLOCK, 1), lambda s, first: (s, 0)),
            pl.BlockSpec(memory_space=pl.ANY),
            pl.BlockSpec(memory_space=pl.ANY),
            pl.BlockSpec(memory_space=pl.ANY),
        ],
        out_specs=pl.BlockSpec((QUERY_BLOCK, width), lambda s, first: (s, 0)),
        scratch_shapes=[
            pltpu.VMEM((3 * rows, 2 * HEAD_SIZE), jnp.bfloat16),
            pltpu.SemaphoreType.DMA((3,)),
        ],
    )
    return pl.pallas_call(
        attend_kernel,
        grid_spec=spec,
        out_shape=jax.ShapeDtypeStruct((rows, width), jnp.bfloat16),
        compiler_params=pltpu.CompilerParams(vmem_limit_bytes=32 * 1024 * 1024),
        cost_estimate=pl.CostEstimate(
            flops=4 * rows * rows * width * 2, bytes_accessed=2 * 6 * rows * width, transcendentals=0
        ),
    )(first, q, low, kv2, kv1, kv0)


def normalize(tokens, norm_gain):
    widened = tokens.astype(jnp.float32)
    mean_sq = jnp.mean(widened * widened, axis=-1, keepdims=True)
    return (widened * lax.rsqrt(mean_sq + 1e-05) * norm_gain.astype(jnp.float32)).astype(
        jnp.bfloat16
    )


def on_device(
    tokens, norm_gain, w_query, key_projection_weight, value_projection_weight, documents
):
    rows = tokens.shape[0]
    me = lax.axis_index("attn")
    mine = jnp.concatenate([key_projection_weight, value_projection_weight, w_query], 1)
    weights = lax.all_gather(mine, "rows", axis=0, tiled=True)

    normed = normalize(tokens, norm_gain)
    cosine, sine = rotary_tables(me * rows + jnp.arange(rows, dtype=jnp.int32))
    doc_ids = documents[0]
    my_docs = lax.dynamic_slice_in_dim(doc_ids, me * rows, rows)
    begin = jnp.sum((doc_ids[None, :] < my_docs[:, None]).astype(jnp.int32), axis=1, keepdims=True)
    low = jnp.maximum(begin - (me - 2) * rows, 0)

    kv = project(normed, weights[:, : 2 * HEAD_SIZE], cosine, sine, 1)
    kv1 = lax.ppermute(kv, "attn", [(0, 1), (1, 2), (2, 3)])
    kv2 = lax.ppermute(kv, "attn", [(0, 2), (1, 3)])
    q = project(normed, weights[:, 2 * HEAD_SIZE :], cosine, sine, 4)
    return attend(q, low, kv2, kv1, kv)


def solution(mesh):
    placed = (
        P(("rows", "attn"), None),
        P(),
        P("rows", "tp"),
        P("rows", "tp"),
        P("rows", "tp"),
        P("rows", None),
    )
    return jax.shard_map(
        on_device, mesh=mesh, in_specs=placed, out_specs=P(("rows", "attn"), "tp"), check_vma=False
    )
```

```python
import functools
import math

import jax
import jax.numpy as jnp
from jax import lax
from jax.experimental import pallas as pl
from jax.experimental.pallas import tpu as pltpu
from jax.sharding import PartitionSpec as P

HEAD_SIZE = 128
KEY_BLOCK = 256
QUERY_BLOCK = 128


def rotary_tables(positions):
    half_dim = HEAD_SIZE // 2
    frequency = jnp.exp(
        jnp.arange(half_dim, dtype=jnp.float32) * (-2.0 * math.log(500000.0) / HEAD_SIZE)
    )
    angles = positions.astype(jnp.float32)[:, None] * frequency[None, :]
    cosine, sine = jnp.cos(angles), jnp.sin(angles)
    return jnp.concatenate([cosine, cosine], 1), jnp.concatenate([-sine, sine], 1)


def project_kernel(rotated_heads, x_ref, w_ref, cos_ref, sin_ref, out_ref, acc_ref):
    step = pl.program_id(0)
    part = jnp.dot(x_ref[...], w_ref[...], preferred_element_type=jnp.float32)

    @pl.when(step == 0)
    def _():
        acc_ref[...] = part

    @pl.when(step > 0)
    def _():
        acc_ref[...] += part

    @pl.when(step == pl.num_programs(0) - 1)
    def _():
        for head in range(out_ref.shape[1] // HEAD_SIZE):
            lanes = slice(head * HEAD_SIZE, (head + 1) * HEAD_SIZE)
            u = acc_ref[:, lanes]
            if head < rotated_heads:
                u = u * cos_ref[...] + pltpu.roll(u, HEAD_SIZE // 2, 1) * sin_ref[...]
            out_ref[:, lanes] = u.astype(jnp.bfloat16)


def project(x, w, cosine, sine, rotated_heads, steps=4):
    rows, depth = x.shape
    width = w.shape[1]
    chunk = depth // steps
    return pl.pallas_call(
        functools.partial(project_kernel, rotated_heads),
        grid=(steps,),
        in_specs=[
            pl.BlockSpec((rows, chunk), lambda s: (0, s)),
            pl.BlockSpec((chunk, width), lambda s: (s, 0)),
            pl.BlockSpec((rows, HEAD_SIZE), lambda s: (0, 0)),
            pl.BlockSpec((rows, HEAD_SIZE), lambda s: (0, 0)),
        ],
        out_specs=pl.BlockSpec((rows, width), lambda s: (0, 0)),
        out_shape=jax.ShapeDtypeStruct((rows, width), jnp.bfloat16),
        scratch_shapes=[pltpu.VMEM((rows, width), jnp.float32)],
        compiler_params=pltpu.CompilerParams(vmem_limit_bytes=60 * 1024 * 1024),
        cost_estimate=pl.CostEstimate(
            flops=2 * rows * depth * width,
            bytes_accessed=2 * (rows * depth + depth * width + rows * width),
            transcendentals=0,
        ),
    )(x, w, cosine, sine)


def attend_kernel(first_ref, q_ref, low_ref, kv2_ref, kv1_ref, kv0_ref, out_ref, kv, sems):
    step = pl.program_id(0)
    rows = kv0_ref.shape[0]
    sources = (kv2_ref, kv1_ref, kv0_ref)

    @pl.when(step == 0)
    def _():
        copies = [
            pltpu.make_async_copy(src, kv.at[pl.ds(n * rows, rows)], sems.at[n])
            for n, src in enumerate(sources)
        ]
        for copy in copies:
            copy.start()
        for copy in copies:
            copy.wait()

    heads = q_ref.shape[1] // HEAD_SIZE
    block = q_ref.shape[0]
    q = jnp.concatenate(
        [q_ref[:, h * HEAD_SIZE : (h + 1) * HEAD_SIZE] for h in range(heads)], axis=0
    )
    low = low_ref[...]
    first_query = 2 * rows + step * block
    query_at = first_query + lax.broadcasted_iota(jnp.int32, (block, KEY_BLOCK), 0)
    lane = lax.broadcasted_iota(jnp.int32, (block, KEY_BLOCK), 1)
    to_log2 = math.log2(math.e) / math.sqrt(HEAD_SIZE)

    def visit(n, carry):
        run_max, run_sum, run_acc = carry
        start = pl.multiple_of(n * KEY_BLOCK, KEY_BLOCK)
        keys = kv[pl.ds(start, KEY_BLOCK), :HEAD_SIZE]
        values = kv[pl.ds(start, KEY_BLOCK), HEAD_SIZE:]
        scores = lax.dot_general(
            q, keys, (((1,), (1,)), ((), ())), preferred_element_type=jnp.float32
        )
        key_at = start + lane
        visible = (key_at >= low) & (key_at <= query_at)
        scores = jnp.where(visible[None], scores.reshape(heads, block, KEY_BLOCK), -1e30)
        scores = scores.reshape(heads * block, KEY_BLOCK)
        new_max = jnp.maximum(run_max, jnp.max(scores, axis=-1, keepdims=True))
        factor = jnp.exp2((run_max - new_max) * to_log2)
        weights = jnp.exp2((scores - new_max) * to_log2)
        run_sum = run_sum * factor + jnp.sum(weights, axis=-1, keepdims=True)
        run_acc = run_acc * factor + jnp.dot(
            weights.astype(jnp.bfloat16), values, preferred_element_type=jnp.float32
        )
        return new_max, run_sum, run_acc

    initial = (
        jnp.full((heads * block, 1), -1e30, jnp.float32),
        jnp.zeros((heads * block, 1), jnp.float32),
        jnp.zeros((heads * block, HEAD_SIZE), jnp.float32),
    )
    last = (first_query + block - 1) // KEY_BLOCK + 1
    _, run_sum, run_acc = lax.fori_loop(first_ref[step], last, visit, initial)
    mixed = (run_acc / run_sum).astype(jnp.bfloat16)
    for h in range(heads):
        out_ref[:, h * HEAD_SIZE : (h + 1) * HEAD_SIZE] = mixed[h * block : (h + 1) * block]


def attend(q, low, kv2, kv1, kv0):
    rows, width = q.shape
    first = low[:: QUERY_BLOCK, 0] // KEY_BLOCK
    spec = pltpu.PrefetchScalarGridSpec(
        num_scalar_prefetch=1,
        grid=(rows // QUERY_BLOCK,),
        in_specs=[
            pl.BlockSpec((QUERY_BLOCK, width), lambda s, first: (s, 0)),
            pl.BlockSpec((QUERY_BLOCK, 1), lambda s, first: (s, 0)),
            pl.BlockSpec(memory_space=pl.ANY),
            pl.BlockSpec(memory_space=pl.ANY),
            pl.BlockSpec(memory_space=pl.ANY),
        ],
        out_specs=pl.BlockSpec((QUERY_BLOCK, width), lambda s, first: (s, 0)),
        scratch_shapes=[
            pltpu.VMEM((3 * rows, 2 * HEAD_SIZE), jnp.bfloat16),
            pltpu.SemaphoreType.DMA((3,)),
        ],
    )
    return pl.pallas_call(
        attend_kernel,
        grid_spec=spec,
        out_shape=jax.ShapeDtypeStruct((rows, width), jnp.bfloat16),
        compiler_params=pltpu.CompilerParams(vmem_limit_bytes=32 * 1024 * 1024),
        cost_estimate=pl.CostEstimate(
            flops=4 * rows * rows * width * 2, bytes_accessed=2 * 6 * rows * width, transcendentals=0
        ),
    )(first, q, low, kv2, kv1, kv0)


def normalize(tokens, norm_gain):
    widened = tokens.astype(jnp.float32)
    mean_sq = jnp.mean(widened * widened, axis=-1, keepdims=True)
    return (widened * lax.rsqrt(mean_sq + 1e-05) * norm_gain.astype(jnp.float32)).astype(
        jnp.bfloat16
    )


def gather_key_value(mine):
    me = lax.axis_index("attn")
    parts = lax.axis_size("attn")
    devices = lax.axis_size("rows")
    rows, width = mine.shape
    quarter = rows // parts
    own = lax.dynamic_slice_in_dim(mine, me * quarter, quarter, 0)
    chips = devices // 2
    same_core = [[2 * z + c for z in range(chips)] for c in range(2)]
    column = lax.all_gather(own, "rows", axis=0, tiled=True, axis_index_groups=same_core)
    spread = jnp.broadcast_to(column[None], (parts, chips * quarter, width))
    half = lax.all_to_all(spread, "attn", 0, 0, tiled=True)
    half = half.reshape(parts, chips, quarter, width).transpose(1, 0, 2, 3)
    half = half.reshape(chips, rows, width)
    other = lax.ppermute(half, "rows", [(i, i ^ 1) for i in range(devices)])
    first = lax.axis_index("rows") % 2 == 0
    both = jnp.stack([jnp.where(first, half, other), jnp.where(first, other, half)], 1)
    return both.reshape(devices * rows, width)


def on_device(
    tokens, norm_gain, w_query, key_projection_weight, value_projection_weight, documents
):
    rows = tokens.shape[0]
    me = lax.axis_index("attn")
    query_weights = lax.all_gather(w_query, "rows", axis=0, tiled=True)
    kv_weights = gather_key_value(
        jnp.concatenate([key_projection_weight, value_projection_weight], 1)
    )

    normed = normalize(tokens, norm_gain)
    cosine, sine = rotary_tables(me * rows + jnp.arange(rows, dtype=jnp.int32))
    doc_ids = documents[0]
    my_docs = lax.dynamic_slice_in_dim(doc_ids, me * rows, rows)
    begin = jnp.sum((doc_ids[None, :] < my_docs[:, None]).astype(jnp.int32), axis=1, keepdims=True)
    low = jnp.maximum(begin - (me - 2) * rows, 0)

    kv = project(normed, kv_weights, cosine, sine, 1)
    kv1 = lax.ppermute(kv, "attn", [(0, 1), (1, 2), (2, 3)])
    kv2 = lax.ppermute(kv, "attn", [(0, 2), (1, 3)])
    q = project(normed, query_weights, cosine, sine, 4)
    return attend(q, low, kv2, kv1, kv)


def solution(mesh):
    placed = (
        P(("rows", "attn"), None),
        P(),
        P("rows", "tp"),
        P("rows", "tp"),
        P("rows", "tp"),
        P("rows", None),
    )
    return jax.shard_map(
        on_device, mesh=mesh, in_specs=placed, out_specs=P(("rows", "attn"), "tp"), check_vma=False
    )
```

```python
import functools
import math

import jax
import jax.numpy as jnp
from jax import lax
from jax.experimental import pallas as pl
from jax.experimental.pallas import tpu as pltpu
from jax.sharding import PartitionSpec as P

HEAD_SIZE = 128
KEY_BLOCK = 256
QUERY_BLOCK = 128


def rotary_tables(positions):
    half_dim = HEAD_SIZE // 2
    frequency = jnp.exp(
        jnp.arange(half_dim, dtype=jnp.float32) * (-2.0 * math.log(500000.0) / HEAD_SIZE)
    )
    angles = positions.astype(jnp.float32)[:, None] * frequency[None, :]
    cosine, sine = jnp.cos(angles), jnp.sin(angles)
    return jnp.concatenate([cosine, cosine], 1), jnp.concatenate([-sine, sine], 1)


def project_kernel(rotated_heads, core_ref, x_ref, wa_ref, wb_ref, cos_ref, sin_ref, out_ref, acc_ref):
    step = pl.program_id(0)
    first = core_ref[0] == 0
    wa, wb = wa_ref[...], wb_ref[...]
    evens, odds = jnp.where(first, wa, wb), jnp.where(first, wb, wa)
    blocks = []
    for n in range(0, wa.shape[0], 128):
        blocks += [evens[n : n + 128], odds[n : n + 128]]
    part = jnp.dot(
        x_ref[...], jnp.concatenate(blocks, axis=0), preferred_element_type=jnp.float32
    )

    @pl.when(step == 0)
    def _():
        acc_ref[...] = part

    @pl.when(step > 0)
    def _():
        acc_ref[...] += part

    @pl.when(step == pl.num_programs(0) - 1)
    def _():
        for head in range(out_ref.shape[1] // HEAD_SIZE):
            lanes = slice(head * HEAD_SIZE, (head + 1) * HEAD_SIZE)
            u = acc_ref[:, lanes]
            if head < rotated_heads:
                u = u * cos_ref[...] + pltpu.roll(u, HEAD_SIZE // 2, 1) * sin_ref[...]
            out_ref[:, lanes] = u.astype(jnp.bfloat16)


def project(core, x, w, cosine, sine, rotated_heads, steps=4):
    rows, depth = x.shape
    width = w[0].shape[1]
    chunk = depth // steps
    w_spec = pl.BlockSpec((chunk // 2, width), lambda s: (s, 0))
    table = pl.BlockSpec((rows, HEAD_SIZE), lambda s: (0, 0))
    return pl.pallas_call(
        functools.partial(project_kernel, rotated_heads),
        grid=(steps,),
        in_specs=[
            pl.BlockSpec(memory_space=pltpu.SMEM),
            pl.BlockSpec((rows, chunk), lambda s: (0, s)),
            w_spec,
            w_spec,
            table,
            table,
        ],
        out_specs=pl.BlockSpec((rows, width), lambda s: (0, 0)),
        out_shape=jax.ShapeDtypeStruct((rows, width), jnp.bfloat16),
        scratch_shapes=[pltpu.VMEM((rows, width), jnp.float32)],
        compiler_params=pltpu.CompilerParams(vmem_limit_bytes=20 * 1024 * 1024),
        cost_estimate=pl.CostEstimate(
            flops=2 * rows * depth * width,
            bytes_accessed=2 * (rows * depth + depth * width + rows * width),
            transcendentals=0,
        ),
    )(core, x, *w, cosine, sine)


def attend_kernel(first_ref, q_ref, low_ref, kv2_ref, kv1_ref, kv0_ref, out_ref, kv, sems):
    step = pl.program_id(0)
    rows = kv0_ref.shape[0]
    sources = (kv2_ref, kv1_ref, kv0_ref)

    @pl.when(step == 0)
    def _():
        copies = [
            pltpu.make_async_copy(src, kv.at[pl.ds(n * rows, rows)], sems.at[n])
            for n, src in enumerate(sources)
        ]
        for copy in copies:
            copy.start()
        for copy in copies:
            copy.wait()

    heads = q_ref.shape[1] // HEAD_SIZE
    block = q_ref.shape[0]
    q = jnp.concatenate(
        [q_ref[:, h * HEAD_SIZE : (h + 1) * HEAD_SIZE] for h in range(heads)], axis=0
    )
    low = low_ref[...]
    first_query = 2 * rows + step * block
    query_at = first_query + lax.broadcasted_iota(jnp.int32, (block, KEY_BLOCK), 0)
    lane = lax.broadcasted_iota(jnp.int32, (block, KEY_BLOCK), 1)
    to_log2 = math.log2(math.e) / math.sqrt(HEAD_SIZE)

    def visit(n, carry):
        run_max, run_sum, run_acc = carry
        start = pl.multiple_of(n * KEY_BLOCK, KEY_BLOCK)
        keys = kv[pl.ds(start, KEY_BLOCK), :HEAD_SIZE]
        values = kv[pl.ds(start, KEY_BLOCK), HEAD_SIZE:]
        scores = lax.dot_general(
            q, keys, (((1,), (1,)), ((), ())), preferred_element_type=jnp.float32
        )
        key_at = start + lane
        visible = (key_at >= low) & (key_at <= query_at)
        scores = jnp.where(visible[None], scores.reshape(heads, block, KEY_BLOCK), -1e30)
        scores = scores.reshape(heads * block, KEY_BLOCK)
        new_max = jnp.maximum(run_max, jnp.max(scores, axis=-1, keepdims=True))
        factor = jnp.exp2((run_max - new_max) * to_log2)
        weights = jnp.exp2((scores - new_max) * to_log2)
        run_sum = run_sum * factor + jnp.sum(weights, axis=-1, keepdims=True)
        run_acc = run_acc * factor + jnp.dot(
            weights.astype(jnp.bfloat16), values, preferred_element_type=jnp.float32
        )
        return new_max, run_sum, run_acc

    initial = (
        jnp.full((heads * block, 1), -1e30, jnp.float32),
        jnp.zeros((heads * block, 1), jnp.float32),
        jnp.zeros((heads * block, HEAD_SIZE), jnp.float32),
    )
    last = (first_query + block - 1) // KEY_BLOCK + 1
    _, run_sum, run_acc = lax.fori_loop(first_ref[step], last, visit, initial)
    mixed = (run_acc / run_sum).astype(jnp.bfloat16)
    for h in range(heads):
        out_ref[:, h * HEAD_SIZE : (h + 1) * HEAD_SIZE] = mixed[h * block : (h + 1) * block]


def attend(q, low, kv2, kv1, kv0):
    rows, width = q.shape
    first = low[:: QUERY_BLOCK, 0] // KEY_BLOCK
    spec = pltpu.PrefetchScalarGridSpec(
        num_scalar_prefetch=1,
        grid=(rows // QUERY_BLOCK,),
        in_specs=[
            pl.BlockSpec((QUERY_BLOCK, width), lambda s, first: (s, 0)),
            pl.BlockSpec((QUERY_BLOCK, 1), lambda s, first: (s, 0)),
            pl.BlockSpec(memory_space=pl.ANY),
            pl.BlockSpec(memory_space=pl.ANY),
            pl.BlockSpec(memory_space=pl.ANY),
        ],
        out_specs=pl.BlockSpec((QUERY_BLOCK, width), lambda s, first: (s, 0)),
        scratch_shapes=[
            pltpu.VMEM((3 * rows, 2 * HEAD_SIZE), jnp.bfloat16),
            pltpu.SemaphoreType.DMA((3,)),
        ],
    )
    return pl.pallas_call(
        attend_kernel,
        grid_spec=spec,
        out_shape=jax.ShapeDtypeStruct((rows, width), jnp.bfloat16),
        compiler_params=pltpu.CompilerParams(vmem_limit_bytes=16 * 1024 * 1024),
        cost_estimate=pl.CostEstimate(
            flops=4 * rows * rows * width * 2, bytes_accessed=2 * 6 * rows * width, transcendentals=0
        ),
    )(first, q, low, kv2, kv1, kv0)


def normalize(tokens, norm_gain):
    widened = tokens.astype(jnp.float32)
    mean_sq = jnp.mean(widened * widened, axis=-1, keepdims=True)
    return (widened * lax.rsqrt(mean_sq + 1e-05) * norm_gain.astype(jnp.float32)).astype(
        jnp.bfloat16
    )


def chip_shift(x, steps):
    n = lax.axis_size("rows") // 2
    pairs = [(2 * z + c, 2 * ((z + steps(z)) % n) + c) for z in range(n) for c in range(2)]
    return lax.ppermute(x, "rows", pairs)


def neighbours(x):
    return [
        x,
        chip_shift(x, lambda z: 1),
        chip_shift(x, lambda z: -1),
        chip_shift(x, lambda z: 2 if z % 2 == 0 else -2),
    ]


def round_attn(spread):
    return lax.all_to_all(spread, "attn", 0, 0, tiled=True)


def columns_kernel(first, here_ref, there_ref, *refs):
    spread_ref, far_ref = refs[-2:]
    take = pl.ds(first, far_ref.shape[-1])
    for n in range(spread_ref.shape[0]):
        spread_ref[n] = here_ref[..., take]
    far_ref[...] = there_ref[..., take]


def columns(here, there, first, width, after):
    whole = pl.BlockSpec(memory_space=pltpu.VMEM)
    one = jax.ShapeDtypeStruct((*here.shape[:-1], width), here.dtype)
    return pl.pallas_call(
        functools.partial(columns_kernel, first),
        in_specs=[whole, whole] + [pl.BlockSpec(memory_space=pl.ANY)] * len(after),
        out_specs=[whole, whole],
        out_shape=[jax.ShapeDtypeStruct((4, *one.shape), one.dtype), one],
        compiler_params=pltpu.CompilerParams(vmem_limit_bytes=8 * 1024 * 1024),
        cost_estimate=pl.CostEstimate(flops=0, bytes_accessed=14 * one.size, transcendentals=0),
    )(here, there, *after)


def order_kernel(place_ref, near_ref, r0_ref, r1_ref, r2_ref, r3_ref, after_ref, out_ref, sems):
    copies = []
    for k in range(4):
        for r in range(4):
            copies.append((near_ref.at[k, r], out_ref.at[:, r, k, 0]))
        for d, ref in enumerate((r0_ref, r1_ref, r2_ref, r3_ref)):
            copies.append((ref.at[k], out_ref.at[:, place_ref[d], k, 1]))
    copies = [
        pltpu.make_async_copy(src, dst, sems.at[n]) for n, (src, dst) in enumerate(copies)
    ]
    for copy in copies:
        copy.start()
    for copy in copies:
        copy.wait()


def in_order(place, near, far, after):
    block, width = near.shape[-2:]
    out = pl.pallas_call(
        order_kernel,
        in_specs=[pl.BlockSpec(memory_space=pltpu.SMEM)] + [pl.BlockSpec(memory_space=pl.ANY)] * 6,
        out_specs=pl.BlockSpec(memory_space=pl.ANY),
        out_shape=jax.ShapeDtypeStruct((4, 4, 4, 2, block, width), jnp.bfloat16),
        scratch_shapes=[pltpu.SemaphoreType.DMA((32,))],
        compiler_params=pltpu.CompilerParams(vmem_limit_bytes=2 * 1024 * 1024),
        cost_estimate=pl.CostEstimate(flops=0, bytes_accessed=4 * near.size * 2, transcendentals=0),
    )(place, near, *far, after)
    return out.reshape(128 * block, width)


def gather_first(mine):
    me = lax.axis_index("attn")
    rows = mine.shape[0]
    quarter = rows // 4
    own = lax.dynamic_slice_in_dim(mine, me * quarter, quarter, 0)
    apart = [[2 * (4 * q + r) + c for q in range(4)] for r in range(4) for c in range(2)]
    close = [[2 * (4 * q + r) + c for r in range(4)] for q in range(4) for c in range(2)]
    far = lax.all_gather(own, "rows", axis=0, tiled=False, axis_index_groups=apart)
    there = round_attn(jnp.broadcast_to(far[None, :, quarter // 2 :], (4, 4, quarter // 2, mine.shape[1])))
    here = lax.all_gather(
        far[:, : quarter // 2], "rows", axis=0, tiled=False, axis_index_groups=close
    )
    return here, there


def swap_cores(own):
    devices = lax.axis_size("rows")
    return own, lax.ppermute(own, "rows", [(i, i ^ 1) for i in range(devices)])


def gather_second(here, there, first, width, after):
    spread, far = columns(here, there, first, width, after)
    return round_attn(spread), neighbours(far)


def on_device(
    tokens, norm_gain, w_query, key_projection_weight, value_projection_weight, documents
):
    rows = tokens.shape[0]
    me = lax.axis_index("attn")
    chip, core = lax.axis_index("rows") // 2, lax.axis_index("rows") % 2
    split = 2 * key_projection_weight.shape[1]
    mine = jnp.concatenate([key_projection_weight, value_projection_weight, w_query], 1)
    here, there = gather_first(mine)
    across = jnp.where(chip % 2 == 0, -2, 2)
    place = (chip + jnp.stack([0 * across, across * 0 - 1, across * 0 + 1, across])) % 4
    place = place.astype(jnp.int32)

    x = normalize(tokens, norm_gain)
    cosine, sine = rotary_tables(me * rows + jnp.arange(rows, dtype=jnp.int32))
    doc_ids = documents[0]
    my_docs = lax.dynamic_slice_in_dim(doc_ids, me * rows, rows)
    begin = jnp.sum((doc_ids[None, :] < my_docs[:, None]).astype(jnp.int32), axis=1, keepdims=True)
    low = jnp.maximum(begin - (me - 2) * rows, 0)

    core = core.reshape(1).astype(jnp.int32)
    near, far = gather_second(here, there, 0, split, [])
    near_q, far_q = gather_second(
        here, there, split, w_query.shape[1], [near, *far[1:], x]
    )
    kv_weights = swap_cores(in_order(place, near, far, x))
    kv = project(core, x, kv_weights, cosine, sine, 1)
    kv1 = lax.ppermute(kv, "attn", [(0, 1), (1, 2), (2, 3)])
    kv2 = lax.ppermute(kv, "attn", [(0, 2), (1, 3)])
    query_weights = swap_cores(in_order(place, near_q, far_q, kv))
    q = project(core, x, query_weights, cosine, sine, 4)
    return attend(q, low, kv2, kv1, kv)


def solution(mesh):
    placed = (
        P(("rows", "attn"), None),
        P(),
        P("rows", "tp"),
        P("rows", "tp"),
        P("rows", "tp"),
        P("rows", None),
    )
    return jax.shard_map(
        on_device, mesh=mesh, in_specs=placed, out_specs=P(("rows", "attn"), "tp"), check_vma=False
    )
```

```python
import functools
import math

import jax
import jax.numpy as jnp
from jax import lax
from jax.experimental import pallas as pl
from jax.experimental.pallas import tpu as pltpu
from jax.sharding import PartitionSpec as P

HEAD_SIZE = 128
KEY_BLOCK = 256
QUERY_BLOCK = 128


def rotary_tables(positions):
    half_dim = HEAD_SIZE // 2
    frequency = jnp.exp(
        jnp.arange(half_dim, dtype=jnp.float32) * (-2.0 * math.log(500000.0) / HEAD_SIZE)
    )
    angles = positions.astype(jnp.float32)[:, None] * frequency[None, :]
    cosine, sine = jnp.cos(angles), jnp.sin(angles)
    return jnp.concatenate([cosine, cosine], 1), jnp.concatenate([-sine, sine], 1)


def rotate(u, cosine, sine):
    return u * cosine + pltpu.roll(u, HEAD_SIZE // 2, 1) * sine


def kv_kernel(core_ref, x_ref, wa_ref, wb_ref, cos_ref, sin_ref, out_ref, acc_ref):
    step = pl.program_id(0)
    first = core_ref[0] == 0
    rows = []
    for chip in range(wa_ref.shape[1]):
        own = jnp.concatenate([wa_ref[k, chip] for k in range(wa_ref.shape[0])], axis=0)
        other = jnp.concatenate([wb_ref[k, chip] for k in range(wb_ref.shape[0])], axis=0)
        rows += [jnp.where(first, own, other), jnp.where(first, other, own)]
    part = jnp.dot(x_ref[...], jnp.concatenate(rows, axis=0), preferred_element_type=jnp.float32)

    @pl.when(step == 0)
    def _():
        acc_ref[...] = part

    @pl.when(step > 0)
    def _():
        acc_ref[...] += part

    @pl.when(step == pl.num_programs(0) - 1)
    def _():
        keys = rotate(acc_ref[:, :HEAD_SIZE], cos_ref[...], sin_ref[...])
        out_ref[:, :HEAD_SIZE] = keys.astype(jnp.bfloat16)
        out_ref[:, HEAD_SIZE:] = acc_ref[:, HEAD_SIZE:].astype(jnp.bfloat16)


def project_kv(core, x, wa, wb, cosine, sine, steps=4):
    rows, depth = x.shape
    quarters, chips, part, width = wa.shape
    w_spec = pl.BlockSpec((quarters, chips // steps, part, width), lambda s: (0, s, 0, 0))
    table = pl.BlockSpec((rows, HEAD_SIZE), lambda s: (0, 0))
    return pl.pallas_call(
        kv_kernel,
        grid=(steps,),
        in_specs=[
            pl.BlockSpec(memory_space=pltpu.SMEM),
            pl.BlockSpec((rows, depth // steps), lambda s: (0, s)),
            w_spec,
            w_spec,
            table,
            table,
        ],
        out_specs=pl.BlockSpec((rows, width), lambda s: (0, 0)),
        out_shape=jax.ShapeDtypeStruct((rows, width), jnp.bfloat16),
        scratch_shapes=[pltpu.VMEM((rows, width), jnp.float32)],
        compiler_params=pltpu.CompilerParams(vmem_limit_bytes=20 * 1024 * 1024),
        cost_estimate=pl.CostEstimate(
            flops=2 * rows * depth * width,
            bytes_accessed=2 * (rows * depth + depth * width + rows * width),
            transcendentals=0,
        ),
    )(core, x, wa, wb, cosine, sine)


def attend_kernel(
    first_ref, low_ref, x_ref, cos_ref, sin_ref, kv2_ref, kv1_ref, kv0_ref, w_ref,
    out_ref, x, w, q, keys, values, sums, acc, sems,
):
    rows, depth = x_ref.shape
    width = out_ref.shape[1]
    heads = width // HEAD_SIZE
    pieces = sems.shape[1]
    piece = depth // pieces
    copies = []
    for n in range(pieces):
        take = pl.ds(n * piece, piece)
        copies.append(pltpu.make_async_copy(w_ref.at[take], w.at[take], sems.at[0, n]))
        copies[-1].start()
        copies.append(pltpu.make_async_copy(x_ref.at[:, take], x.at[:, take], sems.at[1, n]))
        copies[-1].start()

    for n, ref in enumerate((kv2_ref, kv1_ref, kv0_ref)):
        keys[n * rows : (n + 1) * rows] = ref[:, :HEAD_SIZE]
        values[:, n * rows : (n + 1) * rows] = ref[:, HEAD_SIZE:].T

    for n in range(pieces):
        copies[2 * n].wait()
        copies[2 * n + 1].wait()
        take = slice(n * piece, (n + 1) * piece)
        part = jnp.dot(x[:, take], w[take], preferred_element_type=jnp.float32)
        if n == 0:
            sums[...] = part
        else:
            sums[...] += part
    for h in range(heads):
        lanes = slice(h * HEAD_SIZE, (h + 1) * HEAD_SIZE)
        q[:, lanes] = rotate(sums[:, lanes], cos_ref[...], sin_ref[...]).astype(jnp.bfloat16)

    key_lane = lax.broadcasted_iota(jnp.int32, (KEY_BLOCK, QUERY_BLOCK), 0)
    query_lane = lax.broadcasted_iota(jnp.int32, (KEY_BLOCK, QUERY_BLOCK), 1)
    to_log2 = math.log2(math.e) / math.sqrt(HEAD_SIZE)
    for step in range(rows // QUERY_BLOCK):
        block = slice(step * QUERY_BLOCK, (step + 1) * QUERY_BLOCK)
        queries = jnp.concatenate(
            [q[block, h * HEAD_SIZE : (h + 1) * HEAD_SIZE] for h in range(heads)], axis=0
        )
        low = low_ref[step : step + 1, :]
        first_query = 2 * rows + step * QUERY_BLOCK
        acc[...] = jnp.zeros_like(acc)

        def visit(n, carry):
            run_max, run_sum = carry
            start = pl.multiple_of(n * KEY_BLOCK, KEY_BLOCK)
            scores = lax.dot_general(
                keys[pl.ds(start, KEY_BLOCK)],
                queries,
                (((1,), (1,)), ((), ())),
                preferred_element_type=jnp.float32,
            )
            visible = (start + key_lane >= low) & (start + key_lane <= first_query + query_lane)
            visible = jnp.concatenate([visible] * heads, axis=1)
            scores = jnp.where(visible, scores, -1e30)
            new_max = jnp.maximum(run_max, jnp.max(scores, axis=0, keepdims=True))
            factor = jnp.exp2((run_max - new_max) * to_log2)
            weights = jnp.exp2((scores - new_max) * to_log2)
            run_sum = run_sum * factor + jnp.sum(weights, axis=0, keepdims=True)
            acc[...] = acc[...] * factor + jnp.dot(
                values[:, pl.ds(start, KEY_BLOCK)],
                weights.astype(jnp.bfloat16),
                preferred_element_type=jnp.float32,
            )
            return new_max, run_sum

        initial = (
            jnp.full((1, width), -1e30, jnp.float32),
            jnp.zeros((1, width), jnp.float32),
        )
        last = (first_query + QUERY_BLOCK - 1) // KEY_BLOCK + 1
        _, run_sum = lax.fori_loop(first_ref[step], last, visit, initial)
        mixed = acc[...] / run_sum
        for h in range(heads):
            lanes = slice(h * HEAD_SIZE, (h + 1) * HEAD_SIZE)
            out_ref[block, lanes] = mixed[:, lanes].T.astype(jnp.bfloat16)


def attend(first, low, x, cosine, sine, kv2, kv1, kv0, w, pieces=4):
    rows, depth = x.shape
    width = w.shape[1]
    whole = pl.BlockSpec(memory_space=pltpu.VMEM)
    return pl.pallas_call(
        attend_kernel,
        in_specs=[pl.BlockSpec(memory_space=pltpu.SMEM)]
        + [whole, pl.BlockSpec(memory_space=pl.ANY)]
        + [whole] * 5
        + [pl.BlockSpec(memory_space=pl.ANY)],
        out_specs=whole,
        out_shape=jax.ShapeDtypeStruct((rows, width), jnp.bfloat16),
        scratch_shapes=[
            pltpu.VMEM((rows, depth), jnp.bfloat16),
            pltpu.VMEM((depth, width), jnp.bfloat16),
            pltpu.VMEM((rows, width), jnp.bfloat16),
            pltpu.VMEM((3 * rows, HEAD_SIZE), jnp.bfloat16),
            pltpu.VMEM((HEAD_SIZE, 3 * rows), jnp.bfloat16),
            pltpu.VMEM((rows, width), jnp.float32),
            pltpu.VMEM((HEAD_SIZE, width), jnp.float32),
            pltpu.SemaphoreType.DMA((2, pieces)),
        ],
        compiler_params=pltpu.CompilerParams(vmem_limit_bytes=60 * 1024 * 1024),
        cost_estimate=pl.CostEstimate(
            flops=2 * rows * depth * width + 8 * rows * rows * width,
            bytes_accessed=2 * (rows * depth + depth * width),
            transcendentals=0,
        ),
    )(first, low, x, cosine, sine, kv2, kv1, kv0, w)


def normalize(tokens, norm_gain):
    widened = tokens.astype(jnp.float32)
    mean_sq = jnp.mean(widened * widened, axis=-1, keepdims=True)
    return (widened * lax.rsqrt(mean_sq + 1e-05) * norm_gain.astype(jnp.float32)).astype(
        jnp.bfloat16
    )


def gather_key_value(mine):
    me = lax.axis_index("attn")
    parts = lax.axis_size("attn")
    devices = lax.axis_size("rows")
    rows, width = mine.shape
    quarter = rows // parts
    own = lax.dynamic_slice_in_dim(mine, me * quarter, quarter, 0)
    chips = devices // 2
    same_core = [[2 * z + c for z in range(chips)] for c in range(2)]
    column = lax.all_gather(own, "rows", axis=0, tiled=True, axis_index_groups=same_core)
    spread = jnp.broadcast_to(column[None], (parts, chips * quarter, width))
    half = lax.all_to_all(spread, "attn", 0, 0, tiled=True)
    half = half.reshape(parts, chips, quarter, width)
    return half, lax.ppermute(half, "rows", [(i, i ^ 1) for i in range(devices)])


def on_device(
    tokens, norm_gain, w_query, key_projection_weight, value_projection_weight, documents
):
    rows = tokens.shape[0]
    me = lax.axis_index("attn")
    query_weights = lax.all_gather(w_query, "rows", axis=0, tiled=True)
    kv_weights = gather_key_value(
        jnp.concatenate([key_projection_weight, value_projection_weight], 1)
    )

    normed = normalize(tokens, norm_gain)
    cosine, sine = rotary_tables(me * rows + jnp.arange(rows, dtype=jnp.int32))
    doc_ids = documents[0]
    my_docs = lax.dynamic_slice_in_dim(doc_ids, me * rows, rows)
    begin = jnp.sum((doc_ids[None, :] < my_docs[:, None]).astype(jnp.int32), axis=1)
    low = jnp.maximum(begin - (me - 2) * rows, 0).reshape(-1, QUERY_BLOCK)
    first = low[:, 0] // KEY_BLOCK

    core = (lax.axis_index("rows") % 2).astype(jnp.int32).reshape(1)
    kv = project_kv(core, normed, *kv_weights, cosine, sine)
    kv1 = lax.ppermute(kv, "attn", [(0, 1), (1, 2), (2, 3)])
    kv2 = lax.ppermute(kv, "attn", [(0, 2), (1, 3)])
    return attend(first, low, normed, cosine, sine, kv2, kv1, kv, query_weights)


def solution(mesh):
    placed = (
        P(("rows", "attn"), None),
        P(),
        P("rows", "tp"),
        P("rows", "tp"),
        P("rows", "tp"),
        P("rows", None),
    )
    return jax.shard_map(
        on_device, mesh=mesh, in_specs=placed, out_specs=P(("rows", "attn"), "tp"), check_vma=False
    )
```

```python
import functools
import math

import jax
import jax.numpy as jnp
from jax import lax
from jax.experimental import pallas as pl
from jax.experimental.pallas import tpu as pltpu
from jax.sharding import PartitionSpec as P

HEAD_SIZE = 128
KEY_BLOCK = 512
QUERY_BLOCK = 128


def rotary_tables(positions):
    half_dim = HEAD_SIZE // 2
    frequency = jnp.exp(
        jnp.arange(half_dim, dtype=jnp.float32) * (-2.0 * math.log(500000.0) / HEAD_SIZE)
    )
    angles = positions.astype(jnp.float32)[:, None] * frequency[None, :]
    cosine, sine = jnp.cos(angles), jnp.sin(angles)
    return jnp.concatenate([cosine, cosine], 1), jnp.concatenate([-sine, sine], 1)


def rotate(u, cosine, sine):
    return u * cosine + pltpu.roll(u, HEAD_SIZE // 2, 1) * sine


def kv_kernel(core_ref, x_ref, wa_ref, wb_ref, cos_ref, sin_ref, out_ref, acc_ref):
    step = pl.program_id(0)
    first = core_ref[0] == 0
    rows = []
    for chip in range(wa_ref.shape[1]):
        own = jnp.concatenate([wa_ref[k, chip] for k in range(wa_ref.shape[0])], axis=0)
        other = jnp.concatenate([wb_ref[k, chip] for k in range(wb_ref.shape[0])], axis=0)
        rows += [jnp.where(first, own, other), jnp.where(first, other, own)]
    part = jnp.dot(x_ref[...], jnp.concatenate(rows, axis=0), preferred_element_type=jnp.float32)

    @pl.when(step == 0)
    def _():
        acc_ref[...] = part

    @pl.when(step > 0)
    def _():
        acc_ref[...] += part

    @pl.when(step == pl.num_programs(0) - 1)
    def _():
        keys = rotate(acc_ref[:, :HEAD_SIZE], cos_ref[...], sin_ref[...])
        out_ref[:, :HEAD_SIZE] = keys.astype(jnp.bfloat16)
        out_ref[:, HEAD_SIZE:] = acc_ref[:, HEAD_SIZE:].astype(jnp.bfloat16)


def project_kv(core, x, wa, wb, cosine, sine, steps=4):
    rows, depth = x.shape
    quarters, chips, part, width = wa.shape
    w_spec = pl.BlockSpec((quarters, chips // steps, part, width), lambda s: (0, s, 0, 0))
    table = pl.BlockSpec((rows, HEAD_SIZE), lambda s: (0, 0))
    return pl.pallas_call(
        kv_kernel,
        grid=(steps,),
        in_specs=[
            pl.BlockSpec(memory_space=pltpu.SMEM),
            pl.BlockSpec((rows, depth // steps), lambda s: (0, s)),
            w_spec,
            w_spec,
            table,
            table,
        ],
        out_specs=pl.BlockSpec((rows, width), lambda s: (0, 0)),
        out_shape=jax.ShapeDtypeStruct((rows, width), jnp.bfloat16),
        scratch_shapes=[pltpu.VMEM((rows, width), jnp.float32)],
        compiler_params=pltpu.CompilerParams(vmem_limit_bytes=20 * 1024 * 1024),
        cost_estimate=pl.CostEstimate(
            flops=2 * rows * depth * width,
            bytes_accessed=2 * (rows * depth + depth * width + rows * width),
            transcendentals=0,
        ),
    )(core, x, wa, wb, cosine, sine)


def attend_kernel(
    first_ref, low_ref, x_ref, cos_ref, sin_ref, kv2_ref, kv1_ref, kv0_ref, w_ref,
    out_ref, x, w, cos, sin, q, keys, plain, values, sums, acc, sems,
):
    rows, depth = x_ref.shape
    width = out_ref.shape[1]
    heads = width // HEAD_SIZE
    pieces = (sems.shape[0] - 8) // 2
    piece = depth // pieces
    copies = []

    def bring(src, dst):
        copies.append(pltpu.make_async_copy(src, dst, sems.at[len(copies)]))
        copies[-1].start()

    for n in range(pieces):
        take = pl.ds(n * piece, piece)
        bring(w_ref.at[take], w.at[take])
        bring(x_ref.at[:, take], x.at[:, take])
        if n == 0:
            for at, ref in enumerate((kv2_ref, kv1_ref, kv0_ref)):
                part = pl.ds(at * rows, rows)
                bring(ref.at[:, :HEAD_SIZE], keys.at[part])
                bring(ref.at[:, HEAD_SIZE:], plain.at[part])
            bring(cos_ref, cos)
            bring(sin_ref, sin)
    others = copies[2:10]
    copies = copies[:2] + copies[10:]

    for n in range(pieces):
        copies[2 * n].wait()
        copies[2 * n + 1].wait()
        take = slice(n * piece, (n + 1) * piece)
        part = jnp.dot(x[:, take], w[take], preferred_element_type=jnp.float32)
        if n == 0:
            sums[...] = part
        else:
            sums[...] += part
        if n == 0:
            for copy in others:
                copy.wait()
            for at in range(0, 3 * rows, rows):
                values[:, at : at + rows] = plain[at : at + rows].T
    for h in range(heads):
        lanes = slice(h * HEAD_SIZE, (h + 1) * HEAD_SIZE)
        q[h] = rotate(sums[:, lanes], cos[...], sin[...]).T.astype(jnp.bfloat16)

    key_lane = lax.broadcasted_iota(jnp.int32, (KEY_BLOCK, QUERY_BLOCK), 0)
    query_lane = lax.broadcasted_iota(jnp.int32, (KEY_BLOCK, QUERY_BLOCK), 1)
    to_log2 = math.log2(math.e) / math.sqrt(HEAD_SIZE)
    for step in range(rows // QUERY_BLOCK):
        block = slice(step * QUERY_BLOCK, (step + 1) * QUERY_BLOCK)
        queries = jnp.concatenate(
            [q[h, :, block] for h in range(heads)], axis=1
        )
        low = low_ref[step : step + 1, :]
        first_query = 2 * rows + step * QUERY_BLOCK
        acc[...] = jnp.zeros_like(acc)

        def visit(n, carry):
            run_max, run_sum = carry
            start = pl.multiple_of(n * KEY_BLOCK, KEY_BLOCK)
            scores = jnp.dot(
                keys[pl.ds(start, KEY_BLOCK)], queries, preferred_element_type=jnp.float32
            )
            visible = (start + key_lane >= low) & (start + key_lane <= first_query + query_lane)
            visible = jnp.concatenate([visible] * heads, axis=1)
            scores = jnp.where(visible, scores, -1e30)
            new_max = jnp.maximum(run_max, jnp.max(scores, axis=0, keepdims=True))
            factor = jnp.exp2((run_max - new_max) * to_log2)
            weights = jnp.exp2((scores - new_max) * to_log2)
            run_sum = run_sum * factor + jnp.sum(weights, axis=0, keepdims=True)
            acc[...] = acc[...] * factor + jnp.dot(
                values[:, pl.ds(start, KEY_BLOCK)],
                weights.astype(jnp.bfloat16),
                preferred_element_type=jnp.float32,
            )
            return new_max, run_sum

        initial = (
            jnp.full((1, width), -1e30, jnp.float32),
            jnp.zeros((1, width), jnp.float32),
        )
        last = (first_query + QUERY_BLOCK - 1) // KEY_BLOCK + 1
        _, run_sum = lax.fori_loop(first_ref[step], last, visit, initial)
        mixed = acc[...] / run_sum
        for h in range(heads):
            lanes = slice(h * HEAD_SIZE, (h + 1) * HEAD_SIZE)
            out_ref[block, lanes] = mixed[:, lanes].T.astype(jnp.bfloat16)


def attend(first, low, x, cosine, sine, kv2, kv1, kv0, w, pieces=8):
    rows, depth = x.shape
    width = w.shape[1]
    whole = pl.BlockSpec(memory_space=pltpu.VMEM)
    return pl.pallas_call(
        attend_kernel,
        in_specs=[pl.BlockSpec(memory_space=pltpu.SMEM)]
        + [whole]
        + [pl.BlockSpec(memory_space=pl.ANY)] * 7,
        out_specs=whole,
        out_shape=jax.ShapeDtypeStruct((rows, width), jnp.bfloat16),
        scratch_shapes=[
            pltpu.VMEM((rows, depth), jnp.bfloat16),
            pltpu.VMEM((depth, width), jnp.bfloat16),
            pltpu.VMEM((rows, HEAD_SIZE), jnp.float32),
            pltpu.VMEM((rows, HEAD_SIZE), jnp.float32),
            pltpu.VMEM((width // HEAD_SIZE, HEAD_SIZE, rows), jnp.bfloat16),
            pltpu.VMEM((3 * rows, HEAD_SIZE), jnp.bfloat16),
            pltpu.VMEM((3 * rows, HEAD_SIZE), jnp.bfloat16),
            pltpu.VMEM((HEAD_SIZE, 3 * rows), jnp.bfloat16),
            pltpu.VMEM((rows, width), jnp.float32),
            pltpu.VMEM((HEAD_SIZE, width), jnp.float32),
            pltpu.SemaphoreType.DMA((2 * pieces + 8,)),
        ],
        compiler_params=pltpu.CompilerParams(vmem_limit_bytes=60 * 1024 * 1024),
        cost_estimate=pl.CostEstimate(
            flops=2 * rows * depth * width + 8 * rows * rows * width,
            bytes_accessed=2 * (rows * depth + depth * width),
            transcendentals=0,
        ),
    )(first, low, x, cosine, sine, kv2, kv1, kv0, w)


def normalize(tokens, norm_gain):
    widened = tokens.astype(jnp.float32)
    mean_sq = jnp.mean(widened * widened, axis=-1, keepdims=True)
    return (widened * lax.rsqrt(mean_sq + 1e-05) * norm_gain.astype(jnp.float32)).astype(
        jnp.bfloat16
    )


def gather_key_value(mine):
    me = lax.axis_index("attn")
    parts = lax.axis_size("attn")
    devices = lax.axis_size("rows")
    rows, width = mine.shape
    quarter = rows // parts
    own = lax.dynamic_slice_in_dim(mine, me * quarter, quarter, 0)
    chips = devices // 2
    same_core = [[2 * z + c for z in range(chips)] for c in range(2)]
    column = lax.all_gather(own, "rows", axis=0, tiled=True, axis_index_groups=same_core)
    spread = jnp.broadcast_to(column[None], (parts, chips * quarter, width))
    half = lax.all_to_all(spread, "attn", 0, 0, tiled=True)
    half = half.reshape(parts, chips, quarter, width)
    return half, lax.ppermute(half, "rows", [(i, i ^ 1) for i in range(devices)])


def on_device(
    tokens, norm_gain, w_query, key_projection_weight, value_projection_weight, documents
):
    rows = tokens.shape[0]
    me = lax.axis_index("attn")
    query_weights = lax.all_gather(w_query, "rows", axis=0, tiled=True)
    kv_weights = gather_key_value(
        jnp.concatenate([key_projection_weight, value_projection_weight], 1)
    )

    normed = normalize(tokens, norm_gain)
    cosine, sine = rotary_tables(me * rows + jnp.arange(rows, dtype=jnp.int32))
    doc_ids = documents[0]
    my_docs = lax.dynamic_slice_in_dim(doc_ids, me * rows, rows)
    begin = jnp.sum((doc_ids[None, :] < my_docs[:, None]).astype(jnp.int32), axis=1)
    low = jnp.maximum(begin - (me - 2) * rows, 0).reshape(-1, QUERY_BLOCK)
    first = low[:, 0] // KEY_BLOCK

    core = (lax.axis_index("rows") % 2).astype(jnp.int32).reshape(1)
    kv = project_kv(core, normed, *kv_weights, cosine, sine)
    kv1 = lax.ppermute(kv, "attn", [(0, 1), (1, 2), (2, 3)])
    kv2 = lax.ppermute(kv, "attn", [(0, 2), (1, 3)])
    return attend(first, low, normed, cosine, sine, kv2, kv1, kv, query_weights)


def solution(mesh):
    placed = (
        P(("rows", "attn"), None),
        P(),
        P("rows", "tp"),
        P("rows", "tp"),
        P("rows", "tp"),
        P("rows", None),
    )
    return jax.shard_map(
        on_device, mesh=mesh, in_specs=placed, out_specs=P(("rows", "attn"), "tp"), check_vma=False
    )
```

```python
import functools
import math

import jax
import jax.numpy as jnp
from jax import lax
from jax.experimental import pallas as pl
from jax.experimental.pallas import tpu as pltpu
from jax.sharding import PartitionSpec as P

HEAD_SIZE = 128
KEY_BLOCK = 512
QUERY_BLOCK = 128


def rotary_tables(positions):
    half_dim = HEAD_SIZE // 2
    frequency = jnp.exp(
        jnp.arange(half_dim, dtype=jnp.float32) * (-2.0 * math.log(500000.0) / HEAD_SIZE)
    )
    angles = positions.astype(jnp.float32)[:, None] * frequency[None, :]
    cosine, sine = jnp.cos(angles), jnp.sin(angles)
    return jnp.concatenate([cosine, cosine], 1), jnp.concatenate([-sine, sine], 1)


def rotate(u, cosine, sine):
    return u * cosine + pltpu.roll(u, HEAD_SIZE // 2, 1) * sine


def kv_kernel(core_ref, x_ref, wa_ref, wb_ref, cos_ref, sin_ref, out_ref, acc_ref):
    step = pl.program_id(0)
    first = core_ref[0] == 0
    rows = []
    for chip in range(wa_ref.shape[1]):
        own = jnp.concatenate([wa_ref[k, chip] for k in range(wa_ref.shape[0])], axis=0)
        other = jnp.concatenate([wb_ref[k, chip] for k in range(wb_ref.shape[0])], axis=0)
        rows += [jnp.where(first, own, other), jnp.where(first, other, own)]
    part = jnp.dot(x_ref[...], jnp.concatenate(rows, axis=0), preferred_element_type=jnp.float32)

    @pl.when(step == 0)
    def _():
        acc_ref[...] = part

    @pl.when(step > 0)
    def _():
        acc_ref[...] += part

    @pl.when(step == pl.num_programs(0) - 1)
    def _():
        keys = rotate(acc_ref[:, :HEAD_SIZE], cos_ref[...], sin_ref[...])
        out_ref[:, :HEAD_SIZE] = keys.astype(jnp.bfloat16)
        out_ref[:, HEAD_SIZE:] = acc_ref[:, HEAD_SIZE:].astype(jnp.bfloat16)


def project_kv(core, x, wa, wb, cosine, sine, steps=4):
    rows, depth = x.shape
    quarters, chips, part, width = wa.shape
    w_spec = pl.BlockSpec((quarters, chips // steps, part, width), lambda s: (0, s, 0, 0))
    table = pl.BlockSpec((rows, HEAD_SIZE), lambda s: (0, 0))
    return pl.pallas_call(
        kv_kernel,
        grid=(steps,),
        in_specs=[
            pl.BlockSpec(memory_space=pltpu.SMEM),
            pl.BlockSpec((rows, depth // steps), lambda s: (0, s)),
            w_spec,
            w_spec,
            table,
            table,
        ],
        out_specs=pl.BlockSpec((rows, width), lambda s: (0, 0)),
        out_shape=jax.ShapeDtypeStruct((rows, width), jnp.bfloat16),
        scratch_shapes=[pltpu.VMEM((rows, width), jnp.float32)],
        compiler_params=pltpu.CompilerParams(vmem_limit_bytes=20 * 1024 * 1024),
        cost_estimate=pl.CostEstimate(
            flops=2 * rows * depth * width,
            bytes_accessed=2 * (rows * depth + depth * width + rows * width),
            transcendentals=0,
        ),
    )(core, x, wa, wb, cosine, sine)


def attend_kernel(
    core_ref, first_ref, low_ref, x_ref, cos_ref, sin_ref, kv2_ref, kv1_ref, kv0_ref, wa_ref, wb_ref,
    out_ref, x, w, cos, sin, q, keys, plain, values, sums, acc, sems,
):
    rows, depth = x_ref.shape
    width = out_ref.shape[1]
    heads = width // HEAD_SIZE
    pieces = 4
    quarters, chips = wa_ref.shape[:2]
    count = chips // pieces
    piece = depth // pieces
    copies = []

    def bring(src, dst):
        copies.append(pltpu.make_async_copy(src, dst, sems.at[len(copies)]))
        copies[-1].start()

    ready = []
    for n in range(pieces):
        begin = len(copies)
        some = pl.ds(n * count, count)
        for k in range(quarters):
            bring(wa_ref.at[k, some], w.at[some, core_ref[0], k])
            bring(wb_ref.at[k, some], w.at[some, 1 - core_ref[0], k])
        take = pl.ds(n * piece, piece)
        bring(x_ref.at[:, take], x.at[:, take])
        ready.append(copies[begin:])
        if n == 0:
            begin = len(copies)
            for at, ref in enumerate((kv2_ref, kv1_ref, kv0_ref)):
                part = pl.ds(at * rows, rows)
                bring(ref.at[:, :HEAD_SIZE], keys.at[part])
                bring(ref.at[:, HEAD_SIZE:], plain.at[part])
            bring(cos_ref, cos)
            bring(sin_ref, sin)
            others = copies[begin:]

    for n in range(pieces):
        for copy in ready[n]:
            copy.wait()
        weights = w[n * count : (n + 1) * count].reshape(piece, width)
        part = jnp.dot(
            x[:, n * piece : (n + 1) * piece], weights, preferred_element_type=jnp.float32
        )
        if n == 0:
            sums[...] = part
            for copy in others:
                copy.wait()
            for at in range(0, 3 * rows, rows):
                values[:, at : at + rows] = plain[at : at + rows].T
        else:
            sums[...] += part
    for h in range(heads):
        lanes = slice(h * HEAD_SIZE, (h + 1) * HEAD_SIZE)
        q[h] = rotate(sums[:, lanes], cos[...], sin[...]).T.astype(jnp.bfloat16)

    key_lane = lax.broadcasted_iota(jnp.int32, (KEY_BLOCK, QUERY_BLOCK), 0)
    query_lane = lax.broadcasted_iota(jnp.int32, (KEY_BLOCK, QUERY_BLOCK), 1)
    to_log2 = math.log2(math.e) / math.sqrt(HEAD_SIZE)
    for step in range(rows // QUERY_BLOCK):
        block = slice(step * QUERY_BLOCK, (step + 1) * QUERY_BLOCK)
        queries = jnp.concatenate(
            [q[h, :, block] for h in range(heads)], axis=1
        )
        low = low_ref[step : step + 1, :]
        first_query = 2 * rows + step * QUERY_BLOCK
        acc[...] = jnp.zeros_like(acc)

        def visit(n, carry):
            run_max, run_sum = carry
            start = pl.multiple_of(n * KEY_BLOCK, KEY_BLOCK)
            scores = jnp.dot(
                keys[pl.ds(start, KEY_BLOCK)], queries, preferred_element_type=jnp.float32
            )
            visible = (start + key_lane >= low) & (start + key_lane <= first_query + query_lane)
            visible = jnp.concatenate([visible] * heads, axis=1)
            scores = jnp.where(visible, scores, -1e30)
            new_max = jnp.maximum(run_max, jnp.max(scores, axis=0, keepdims=True))
            factor = jnp.exp2((run_max - new_max) * to_log2)
            weights = jnp.exp2((scores - new_max) * to_log2)
            run_sum = run_sum * factor + jnp.sum(weights, axis=0, keepdims=True)
            acc[...] = acc[...] * factor + jnp.dot(
                values[:, pl.ds(start, KEY_BLOCK)],
                weights.astype(jnp.bfloat16),
                preferred_element_type=jnp.float32,
            )
            return new_max, run_sum

        initial = (
            jnp.full((1, width), -1e30, jnp.float32),
            jnp.zeros((1, width), jnp.float32),
        )
        last = (first_query + QUERY_BLOCK - 1) // KEY_BLOCK + 1
        _, run_sum = lax.fori_loop(first_ref[step], last, visit, initial)
        mixed = acc[...] / run_sum
        for h in range(heads):
            lanes = slice(h * HEAD_SIZE, (h + 1) * HEAD_SIZE)
            out_ref[block, lanes] = mixed[:, lanes].T.astype(jnp.bfloat16)


def attend(core, first, low, x, cosine, sine, kv2, kv1, kv0, wa, wb):
    rows, depth = x.shape
    quarters, chips, part, width = wa.shape
    whole = pl.BlockSpec(memory_space=pltpu.VMEM)
    return pl.pallas_call(
        attend_kernel,
        in_specs=[pl.BlockSpec(memory_space=pltpu.SMEM)] * 2
        + [whole]
        + [pl.BlockSpec(memory_space=pl.ANY)] * 8,
        out_specs=whole,
        out_shape=jax.ShapeDtypeStruct((rows, width), jnp.bfloat16),
        scratch_shapes=[
            pltpu.VMEM((rows, depth), jnp.bfloat16),
            pltpu.VMEM((chips, 2, quarters, part, width), jnp.bfloat16),
            pltpu.VMEM((rows, HEAD_SIZE), jnp.float32),
            pltpu.VMEM((rows, HEAD_SIZE), jnp.float32),
            pltpu.VMEM((width // HEAD_SIZE, HEAD_SIZE, rows), jnp.bfloat16),
            pltpu.VMEM((3 * rows, HEAD_SIZE), jnp.bfloat16),
            pltpu.VMEM((3 * rows, HEAD_SIZE), jnp.bfloat16),
            pltpu.VMEM((HEAD_SIZE, 3 * rows), jnp.bfloat16),
            pltpu.VMEM((rows, width), jnp.float32),
            pltpu.VMEM((HEAD_SIZE, width), jnp.float32),
            pltpu.SemaphoreType.DMA((4 * (2 * quarters + 1) + 8,)),
        ],
        compiler_params=pltpu.CompilerParams(vmem_limit_bytes=60 * 1024 * 1024),
        cost_estimate=pl.CostEstimate(
            flops=2 * rows * depth * width + 8 * rows * rows * width,
            bytes_accessed=2 * (rows * depth + depth * width),
            transcendentals=0,
        ),
    )(core, first, low, x, cosine, sine, kv2, kv1, kv0, wa, wb)


def normalize(tokens, norm_gain):
    widened = tokens.astype(jnp.float32)
    mean_sq = jnp.mean(widened * widened, axis=-1, keepdims=True)
    return (widened * lax.rsqrt(mean_sq + 1e-05) * norm_gain.astype(jnp.float32)).astype(
        jnp.bfloat16
    )


def gather_column(mine):
    quarter = mine.shape[0] // lax.axis_size("attn")
    own = lax.dynamic_slice_in_dim(mine, lax.axis_index("attn") * quarter, quarter, 0)
    chips = lax.axis_size("rows") // 2
    same_core = [[2 * z + c for z in range(chips)] for c in range(2)]
    return lax.all_gather(own, "rows", axis=0, tiled=False, axis_index_groups=same_core)


def nothing_kernel(*refs):
    del refs


def after(x, *others):
    anywhere = pl.BlockSpec(memory_space=pl.ANY)
    return pl.pallas_call(
        nothing_kernel,
        in_specs=[anywhere] * (1 + len(others)),
        out_specs=anywhere,
        out_shape=jax.ShapeDtypeStruct(x.shape, x.dtype),
        input_output_aliases={0: 0},
        compiler_params=pltpu.CompilerParams(vmem_limit_bytes=1024 * 1024),
        cost_estimate=pl.CostEstimate(flops=0, bytes_accessed=0, transcendentals=0),
    )(x, *others)


def columns_kernel(first, x_ref, out_ref):
    for n in range(out_ref.shape[0]):
        out_ref[n] = x_ref[..., first : first + out_ref.shape[-1]]


def spread_attn(x, first, width):
    parts = lax.axis_size("attn")
    whole = pl.BlockSpec(memory_space=pltpu.VMEM)
    out = jax.ShapeDtypeStruct((parts, *x.shape[:-1], width), x.dtype)
    spread = pl.pallas_call(
        functools.partial(columns_kernel, first),
        in_specs=[whole],
        out_specs=whole,
        out_shape=out,
        compiler_params=pltpu.CompilerParams(vmem_limit_bytes=8 * 1024 * 1024),
        cost_estimate=pl.CostEstimate(flops=0, bytes_accessed=3 * out.size, transcendentals=0),
    )(x)
    return lax.all_to_all(spread, "attn", 0, 0, tiled=True)


def swap_cores(half):
    return lax.ppermute(half, "rows", [(i, i ^ 1) for i in range(lax.axis_size("rows"))])


def on_device(
    tokens, norm_gain, w_query, key_projection_weight, value_projection_weight, documents
):
    rows = tokens.shape[0]
    me = lax.axis_index("attn")
    split = 2 * HEAD_SIZE
    column = gather_column(
        jnp.concatenate([key_projection_weight, value_projection_weight, w_query], 1)
    )
    normed = normalize(tokens, norm_gain)
    kv_half = spread_attn(column, 0, split)
    query_half = spread_attn(after(column, normed[:16, :HEAD_SIZE], kv_half), split, w_query.shape[1])
    cosine, sine = rotary_tables(me * rows + jnp.arange(rows, dtype=jnp.int32))
    doc_ids = documents[0]
    my_docs = lax.dynamic_slice_in_dim(doc_ids, me * rows, rows)
    begin = jnp.sum((doc_ids[None, :] < my_docs[:, None]).astype(jnp.int32), axis=1)
    low = jnp.maximum(begin - (me - 2) * rows, 0).reshape(-1, QUERY_BLOCK)
    first = low[:, 0] // KEY_BLOCK

    core = (lax.axis_index("rows") % 2).astype(jnp.int32).reshape(1)
    kv = project_kv(core, normed, kv_half, swap_cores(kv_half), cosine, sine)
    kv1 = lax.ppermute(kv, "attn", [(0, 1), (1, 2), (2, 3)])
    kv2 = lax.ppermute(kv, "attn", [(0, 2), (1, 3)])
    query_half = after(query_half, kv1, kv2)
    other = swap_cores(query_half)
    return attend(core, first, low, normed, cosine, sine, kv2, kv1, kv, query_half, other)


def solution(mesh):
    placed = (
        P(("rows", "attn"), None),
        P(),
        P("rows", "tp"),
        P("rows", "tp"),
        P("rows", "tp"),
        P("rows", None),
    )
    return jax.shard_map(
        on_device, mesh=mesh, in_specs=placed, out_specs=P(("rows", "attn"), "tp"), check_vma=False
    )
```

```python
import functools
import math

import jax
import jax.numpy as jnp
from jax import lax
from jax.experimental import pallas as pl
from jax.experimental.pallas import tpu as pltpu
from jax.sharding import PartitionSpec as P

HEAD_SIZE = 128
KEY_BLOCK = 512
QUERY_BLOCK = 128


def rotary_tables(positions):
    half_dim = HEAD_SIZE // 2
    frequency = jnp.exp(
        jnp.arange(half_dim, dtype=jnp.float32) * (-2.0 * math.log(500000.0) / HEAD_SIZE)
    )
    angles = positions.astype(jnp.float32)[:, None] * frequency[None, :]
    cosine, sine = jnp.cos(angles), jnp.sin(angles)
    return jnp.concatenate([cosine, cosine], 1), jnp.concatenate([-sine, sine], 1)


def rotate(u, cosine, sine):
    return u * cosine + pltpu.roll(u, HEAD_SIZE // 2, 1) * sine


def kv_kernel(core_ref, x_ref, wa_ref, wb_ref, cos_ref, sin_ref, out_ref, acc_ref):
    step = pl.program_id(0)
    first = core_ref[0] == 0
    rows = []
    for chip in range(wa_ref.shape[1]):
        own = jnp.concatenate([wa_ref[k, chip] for k in range(wa_ref.shape[0])], axis=0)
        other = jnp.concatenate([wb_ref[k, chip] for k in range(wb_ref.shape[0])], axis=0)
        rows += [jnp.where(first, own, other), jnp.where(first, other, own)]
    part = jnp.dot(x_ref[...], jnp.concatenate(rows, axis=0), preferred_element_type=jnp.float32)

    @pl.when(step == 0)
    def _():
        acc_ref[...] = part

    @pl.when(step > 0)
    def _():
        acc_ref[...] += part

    @pl.when(step == pl.num_programs(0) - 1)
    def _():
        keys = rotate(acc_ref[:, :HEAD_SIZE], cos_ref[...], sin_ref[...])
        out_ref[:, :HEAD_SIZE] = keys.astype(jnp.bfloat16)
        out_ref[:, HEAD_SIZE:] = acc_ref[:, HEAD_SIZE:].astype(jnp.bfloat16)


def project_kv(core, x, wa, wb, cosine, sine, steps=4):
    rows, depth = x.shape
    quarters, chips, part, width = wa.shape
    w_spec = pl.BlockSpec((quarters, chips // steps, part, width), lambda s: (0, s, 0, 0))
    table = pl.BlockSpec((rows, HEAD_SIZE), lambda s: (0, 0))
    return pl.pallas_call(
        kv_kernel,
        grid=(steps,),
        in_specs=[
            pl.BlockSpec(memory_space=pltpu.SMEM),
            pl.BlockSpec((rows, depth // steps), lambda s: (0, s)),
            w_spec,
            w_spec,
            table,
            table,
        ],
        out_specs=pl.BlockSpec((rows, width), lambda s: (0, 0)),
        out_shape=jax.ShapeDtypeStruct((rows, width), jnp.bfloat16),
        scratch_shapes=[pltpu.VMEM((rows, width), jnp.float32)],
        compiler_params=pltpu.CompilerParams(vmem_limit_bytes=20 * 1024 * 1024),
        cost_estimate=pl.CostEstimate(
            flops=2 * rows * depth * width,
            bytes_accessed=2 * (rows * depth + depth * width + rows * width),
            transcendentals=0,
        ),
    )(core, x, wa, wb, cosine, sine)


def attend_kernel(
    core_ref, first_ref, low_ref, x_ref, cos_ref, sin_ref, kv2_ref, kv1_ref, kv0_ref, wa_ref, wb_ref,
    out_ref, x, w, cos, sin, q, keys, plain, values, sums, acc, sems,
):
    rows, depth = x_ref.shape
    width = out_ref.shape[1]
    heads = width // HEAD_SIZE
    pieces = 4
    quarters, chips = wa_ref.shape[:2]
    count = chips // pieces
    piece = depth // pieces
    copies = []

    def bring(src, dst):
        copies.append(pltpu.make_async_copy(src, dst, sems.at[len(copies)]))
        copies[-1].start()

    ready = []
    for n in range(pieces):
        begin = len(copies)
        some = pl.ds(n * count, count)
        for k in range(quarters):
            bring(wa_ref.at[k, some], w.at[some, core_ref[0], k])
            bring(wb_ref.at[k, some], w.at[some, 1 - core_ref[0], k])
        take = pl.ds(n * piece, piece)
        bring(x_ref.at[:, take], x.at[:, take])
        ready.append(copies[begin:])
        if n == 0:
            begin = len(copies)
            for at, ref in enumerate((kv2_ref, kv1_ref, kv0_ref)):
                part = pl.ds(at * rows, rows)
                bring(ref.at[:, :HEAD_SIZE], keys.at[part])
                bring(ref.at[:, HEAD_SIZE:], plain.at[part])
            bring(cos_ref, cos)
            bring(sin_ref, sin)
            others = copies[begin:]

    for n in range(pieces):
        for copy in ready[n]:
            copy.wait()
        weights = w[n * count : (n + 1) * count].reshape(piece, width)
        part = jnp.dot(
            x[:, n * piece : (n + 1) * piece], weights, preferred_element_type=jnp.float32
        )
        if n == 0:
            sums[...] = part
            for copy in others:
                copy.wait()
            for at in range(0, 3 * rows, rows):
                values[:, at : at + rows] = plain[at : at + rows].T
        else:
            sums[...] += part
    for h in range(heads):
        lanes = slice(h * HEAD_SIZE, (h + 1) * HEAD_SIZE)
        q[h] = rotate(sums[:, lanes], cos[...], sin[...]).T.astype(jnp.bfloat16)

    key_lane = lax.broadcasted_iota(jnp.int32, (KEY_BLOCK, QUERY_BLOCK), 0)
    query_lane = lax.broadcasted_iota(jnp.int32, (KEY_BLOCK, QUERY_BLOCK), 1)
    to_log2 = math.log2(math.e) / math.sqrt(HEAD_SIZE)
    for step in range(rows // QUERY_BLOCK):
        block = slice(step * QUERY_BLOCK, (step + 1) * QUERY_BLOCK)
        queries = jnp.concatenate(
            [q[h, :, block] for h in range(heads)], axis=1
        )
        low = low_ref[step : step + 1, :]
        first_query = 2 * rows + step * QUERY_BLOCK
        acc[...] = jnp.zeros_like(acc)

        def visit(n, carry):
            run_max, run_sum = carry
            start = pl.multiple_of(n * KEY_BLOCK, KEY_BLOCK)
            scores = jnp.dot(
                keys[pl.ds(start, KEY_BLOCK)], queries, preferred_element_type=jnp.float32
            )
            visible = (start + key_lane >= low) & (start + key_lane <= first_query + query_lane)
            visible = jnp.concatenate([visible] * heads, axis=1)
            scores = jnp.where(visible, scores, -1e30)
            new_max = jnp.maximum(run_max, jnp.max(scores, axis=0, keepdims=True))
            factor = jnp.exp2((run_max - new_max) * to_log2)
            weights = jnp.exp2((scores - new_max) * to_log2)
            run_sum = run_sum * factor + jnp.sum(weights, axis=0, keepdims=True)
            acc[...] = acc[...] * factor + jnp.dot(
                values[:, pl.ds(start, KEY_BLOCK)],
                weights.astype(jnp.bfloat16),
                preferred_element_type=jnp.float32,
            )
            return new_max, run_sum

        initial = (
            jnp.full((1, width), -1e30, jnp.float32),
            jnp.zeros((1, width), jnp.float32),
        )
        last = (first_query + QUERY_BLOCK - 1) // KEY_BLOCK + 1
        _, run_sum = lax.fori_loop(first_ref[step], last, visit, initial)
        mixed = acc[...] / run_sum
        for h in range(heads):
            lanes = slice(h * HEAD_SIZE, (h + 1) * HEAD_SIZE)
            out_ref[block, lanes] = mixed[:, lanes].T.astype(jnp.bfloat16)


def attend(core, first, low, x, cosine, sine, kv2, kv1, kv0, wa, wb):
    rows, depth = x.shape
    quarters, chips, part, width = wa.shape
    whole = pl.BlockSpec(memory_space=pltpu.VMEM)
    return pl.pallas_call(
        attend_kernel,
        in_specs=[pl.BlockSpec(memory_space=pltpu.SMEM)] * 2
        + [whole]
        + [pl.BlockSpec(memory_space=pl.ANY)] * 8,
        out_specs=whole,
        out_shape=jax.ShapeDtypeStruct((rows, width), jnp.bfloat16),
        scratch_shapes=[
            pltpu.VMEM((rows, depth), jnp.bfloat16),
            pltpu.VMEM((chips, 2, quarters, part, width), jnp.bfloat16),
            pltpu.VMEM((rows, HEAD_SIZE), jnp.float32),
            pltpu.VMEM((rows, HEAD_SIZE), jnp.float32),
            pltpu.VMEM((width // HEAD_SIZE, HEAD_SIZE, rows), jnp.bfloat16),
            pltpu.VMEM((3 * rows, HEAD_SIZE), jnp.bfloat16),
            pltpu.VMEM((3 * rows, HEAD_SIZE), jnp.bfloat16),
            pltpu.VMEM((HEAD_SIZE, 3 * rows), jnp.bfloat16),
            pltpu.VMEM((rows, width), jnp.float32),
            pltpu.VMEM((HEAD_SIZE, width), jnp.float32),
            pltpu.SemaphoreType.DMA((4 * (2 * quarters + 1) + 8,)),
        ],
        compiler_params=pltpu.CompilerParams(vmem_limit_bytes=60 * 1024 * 1024),
        cost_estimate=pl.CostEstimate(
            flops=2 * rows * depth * width + 8 * rows * rows * width,
            bytes_accessed=2 * (rows * depth + depth * width),
            transcendentals=0,
        ),
    )(core, first, low, x, cosine, sine, kv2, kv1, kv0, wa, wb)


def normalize(tokens, norm_gain):
    widened = tokens.astype(jnp.float32)
    mean_sq = jnp.mean(widened * widened, axis=-1, keepdims=True)
    return (widened * lax.rsqrt(mean_sq + 1e-05) * norm_gain.astype(jnp.float32)).astype(
        jnp.bfloat16
    )


def gather_column(mine):
    quarter = mine.shape[0] // lax.axis_size("attn")
    own = lax.dynamic_slice_in_dim(mine, lax.axis_index("attn") * quarter, quarter, 0)
    chips = lax.axis_size("rows") // 2
    same_core = [[2 * z + c for z in range(chips)] for c in range(2)]
    return lax.all_gather(own, "rows", axis=0, tiled=False, axis_index_groups=same_core)


def nothing_kernel(*refs):
    del refs


def after(x, *others):
    anywhere = pl.BlockSpec(memory_space=pl.ANY)
    return pl.pallas_call(
        nothing_kernel,
        in_specs=[anywhere] * (1 + len(others)),
        out_specs=anywhere,
        out_shape=jax.ShapeDtypeStruct(x.shape, x.dtype),
        input_output_aliases={0: 0},
        compiler_params=pltpu.CompilerParams(vmem_limit_bytes=1024 * 1024),
        cost_estimate=pl.CostEstimate(flops=0, bytes_accessed=0, transcendentals=0),
    )(x, *others)


def columns_kernel(first, x_ref, out_ref):
    for n in range(out_ref.shape[0]):
        out_ref[n] = x_ref[..., first : first + out_ref.shape[-1]]


def spread_attn(x, first, width):
    parts = lax.axis_size("attn")
    whole = pl.BlockSpec(memory_space=pltpu.VMEM)
    out = jax.ShapeDtypeStruct((parts, *x.shape[:-1], width), x.dtype)
    spread = pl.pallas_call(
        functools.partial(columns_kernel, first),
        in_specs=[whole],
        out_specs=whole,
        out_shape=out,
        compiler_params=pltpu.CompilerParams(vmem_limit_bytes=60 * 1024 * 1024),
        cost_estimate=pl.CostEstimate(flops=0, bytes_accessed=3 * out.size, transcendentals=0),
    )(x)
    return lax.all_to_all(spread, "attn", 0, 0, tiled=True)


def swap_cores(half):
    return lax.ppermute(half, "rows", [(i, i ^ 1) for i in range(lax.axis_size("rows"))])


def on_device(
    tokens, norm_gain, w_query, key_projection_weight, value_projection_weight, documents
):
    rows = tokens.shape[0]
    me = lax.axis_index("attn")
    split = 2 * HEAD_SIZE
    column = gather_column(
        jnp.concatenate([key_projection_weight, value_projection_weight, w_query], 1)
    )
    normed = normalize(tokens, norm_gain)
    kv_half = spread_attn(column, 0, split)
    query_half = spread_attn(after(column, normed[:16, :HEAD_SIZE], kv_half), split, w_query.shape[1])
    cosine, sine = rotary_tables(me * rows + jnp.arange(rows, dtype=jnp.int32))
    doc_ids = documents[0]
    my_docs = lax.dynamic_slice_in_dim(doc_ids, me * rows, rows)
    begin = jnp.sum((doc_ids[None, :] < my_docs[:, None]).astype(jnp.int32), axis=1)
    low = jnp.maximum(begin - (me - 2) * rows, 0).reshape(-1, QUERY_BLOCK)
    first = low[:, 0] // KEY_BLOCK

    core = (lax.axis_index("rows") % 2).astype(jnp.int32).reshape(1)
    kv = project_kv(core, normed, kv_half, swap_cores(kv_half), cosine, sine)
    kv1 = lax.ppermute(kv, "attn", [(0, 1), (1, 2), (2, 3)])
    kv2 = lax.ppermute(kv1, "attn", [(1, 2), (2, 3)])
    query_half = after(query_half, kv1)
    other = swap_cores(query_half)
    return attend(core, first, low, normed, cosine, sine, kv2, kv1, kv, query_half, other)


def solution(mesh):
    placed = (
        P(("rows", "attn"), None),
        P(),
        P("rows", "tp"),
        P("rows", "tp"),
        P("rows", "tp"),
        P("rows", None),
    )
    return jax.shard_map(
        on_device, mesh=mesh, in_specs=placed, out_specs=P(("rows", "attn"), "tp"), check_vma=False
    )
```

```python
import functools
import math

import jax
import jax.numpy as jnp
from jax import lax
from jax.experimental import pallas as pl
from jax.experimental.pallas import tpu as pltpu
from jax.sharding import PartitionSpec as P

HEAD_SIZE = 128
KEY_BLOCK = 512
QUERY_BLOCK = 128


def rotary_tables(positions):
    half_dim = HEAD_SIZE // 2
    frequency = jnp.exp(
        jnp.arange(half_dim, dtype=jnp.float32) * (-2.0 * math.log(500000.0) / HEAD_SIZE)
    )
    angles = positions.astype(jnp.float32)[:, None] * frequency[None, :]
    cosine, sine = jnp.cos(angles), jnp.sin(angles)
    return jnp.concatenate([cosine, cosine], 1), jnp.concatenate([-sine, sine], 1)


def rotate(u, cosine, sine):
    return u * cosine + pltpu.roll(u, HEAD_SIZE // 2, 1) * sine


def kv_kernel(core_ref, x_ref, wa_ref, wb_ref, cos_ref, sin_ref, out_ref, acc_ref):
    step = pl.program_id(0)
    first = core_ref[0] == 0
    rows = []
    for chip in range(wa_ref.shape[1]):
        own = jnp.concatenate([wa_ref[k, chip] for k in range(wa_ref.shape[0])], axis=0)
        other = jnp.concatenate([wb_ref[k, chip] for k in range(wb_ref.shape[0])], axis=0)
        rows += [jnp.where(first, own, other), jnp.where(first, other, own)]
    part = jnp.dot(x_ref[...], jnp.concatenate(rows, axis=0), preferred_element_type=jnp.float32)

    @pl.when(step == 0)
    def _():
        acc_ref[...] = part

    @pl.when(step > 0)
    def _():
        acc_ref[...] += part

    @pl.when(step == pl.num_programs(0) - 1)
    def _():
        keys = rotate(acc_ref[:, :HEAD_SIZE], cos_ref[...], sin_ref[...])
        out_ref[:, :HEAD_SIZE] = keys.astype(jnp.bfloat16)
        out_ref[:, HEAD_SIZE:] = acc_ref[:, HEAD_SIZE:].astype(jnp.bfloat16)


def project_kv(core, x, wa, wb, cosine, sine, steps=4):
    rows, depth = x.shape
    quarters, chips, part, width = wa.shape
    w_spec = pl.BlockSpec((quarters, chips // steps, part, width), lambda s: (0, s, 0, 0))
    table = pl.BlockSpec((rows, HEAD_SIZE), lambda s: (0, 0))
    return pl.pallas_call(
        kv_kernel,
        grid=(steps,),
        in_specs=[
            pl.BlockSpec(memory_space=pltpu.SMEM),
            pl.BlockSpec((rows, depth // steps), lambda s: (0, s)),
            w_spec,
            w_spec,
            table,
            table,
        ],
        out_specs=pl.BlockSpec((rows, width), lambda s: (0, 0)),
        out_shape=jax.ShapeDtypeStruct((rows, width), jnp.bfloat16),
        scratch_shapes=[pltpu.VMEM((rows, width), jnp.float32)],
        compiler_params=pltpu.CompilerParams(vmem_limit_bytes=20 * 1024 * 1024),
        cost_estimate=pl.CostEstimate(
            flops=2 * rows * depth * width,
            bytes_accessed=2 * (rows * depth + depth * width + rows * width),
            transcendentals=0,
        ),
    )(core, x, wa, wb, cosine, sine)


def attend_kernel(
    core_ref, first_ref, low_ref, x_ref, cos_ref, sin_ref, kv2_ref, kv1_ref, kv0_ref, wa_ref, wb_ref,
    out_ref, x, w, cos, sin, q, keys, plain, values, sums, acc, sems,
):
    rows, depth = x_ref.shape
    width = out_ref.shape[1]
    heads = width // HEAD_SIZE
    pieces = 4
    quarters, chips = wa_ref.shape[:2]
    count = chips // pieces
    piece = depth // pieces
    copies = []

    def bring(src, dst):
        copies.append(pltpu.make_async_copy(src, dst, sems.at[len(copies)]))
        copies[-1].start()

    ready = []
    for n in range(pieces):
        begin = len(copies)
        some = pl.ds(n * count, count)
        for k in range(quarters):
            bring(wa_ref.at[k, some], w.at[some, core_ref[0], k])
            bring(wb_ref.at[k, some], w.at[some, 1 - core_ref[0], k])
        take = pl.ds(n * piece, piece)
        bring(x_ref.at[:, take], x.at[:, take])
        ready.append(copies[begin:])
        if n == 0:
            begin = len(copies)
            for at, ref in enumerate((kv2_ref, kv1_ref, kv0_ref)):
                part = pl.ds(at * rows, rows)
                bring(ref.at[:, :HEAD_SIZE], keys.at[part])
                bring(ref.at[:, HEAD_SIZE:], plain.at[part])
            bring(cos_ref, cos)
            bring(sin_ref, sin)
            others = copies[begin:]

    for n in range(pieces):
        for copy in ready[n]:
            copy.wait()
        weights = w[n * count : (n + 1) * count].reshape(piece, width)
        part = jnp.dot(
            x[:, n * piece : (n + 1) * piece], weights, preferred_element_type=jnp.float32
        )
        if n == 0:
            sums[...] = part
            for copy in others:
                copy.wait()
            for at in range(0, 3 * rows, rows):
                values[:, at : at + rows] = plain[at : at + rows].T
        else:
            sums[...] += part
    for h in range(heads):
        lanes = slice(h * HEAD_SIZE, (h + 1) * HEAD_SIZE)
        q[h] = rotate(sums[:, lanes], cos[...], sin[...]).T.astype(jnp.bfloat16)

    key_lane = lax.broadcasted_iota(jnp.int32, (KEY_BLOCK, QUERY_BLOCK), 0)
    query_lane = lax.broadcasted_iota(jnp.int32, (KEY_BLOCK, QUERY_BLOCK), 1)
    to_log2 = math.log2(math.e) / math.sqrt(HEAD_SIZE)
    for step in range(rows // QUERY_BLOCK):
        block = slice(step * QUERY_BLOCK, (step + 1) * QUERY_BLOCK)
        queries = jnp.concatenate(
            [q[h, :, block] for h in range(heads)], axis=1
        )
        low = low_ref[step : step + 1, :]
        first_query = 2 * rows + step * QUERY_BLOCK
        acc[...] = jnp.zeros_like(acc)

        def visit(n, carry):
            run_max, run_sum = carry
            start = pl.multiple_of(n * KEY_BLOCK, KEY_BLOCK)
            scores = jnp.dot(
                keys[pl.ds(start, KEY_BLOCK)], queries, preferred_element_type=jnp.float32
            )
            visible = (start + key_lane >= low) & (start + key_lane <= first_query + query_lane)
            visible = jnp.concatenate([visible] * heads, axis=1)
            scores = jnp.where(visible, scores, -1e30)
            new_max = jnp.maximum(run_max, jnp.max(scores, axis=0, keepdims=True))
            factor = jnp.exp2((run_max - new_max) * to_log2)
            weights = jnp.exp2((scores - new_max) * to_log2)
            run_sum = run_sum * factor + jnp.sum(weights, axis=0, keepdims=True)
            acc[...] = acc[...] * factor + jnp.dot(
                values[:, pl.ds(start, KEY_BLOCK)],
                weights.astype(jnp.bfloat16),
                preferred_element_type=jnp.float32,
            )
            return new_max, run_sum

        initial = (
            jnp.full((1, width), -1e30, jnp.float32),
            jnp.zeros((1, width), jnp.float32),
        )
        last = (first_query + QUERY_BLOCK - 1) // KEY_BLOCK + 1
        _, run_sum = lax.fori_loop(first_ref[step], last, visit, initial)
        mixed = acc[...] / run_sum
        for h in range(heads):
            lanes = slice(h * HEAD_SIZE, (h + 1) * HEAD_SIZE)
            out_ref[block, lanes] = mixed[:, lanes].T.astype(jnp.bfloat16)


def attend(core, first, low, x, cosine, sine, kv2, kv1, kv0, wa, wb):
    rows, depth = x.shape
    quarters, chips, part, width = wa.shape
    whole = pl.BlockSpec(memory_space=pltpu.VMEM)
    return pl.pallas_call(
        attend_kernel,
        in_specs=[pl.BlockSpec(memory_space=pltpu.SMEM)] * 2
        + [whole]
        + [pl.BlockSpec(memory_space=pl.ANY)] * 8,
        out_specs=whole,
        out_shape=jax.ShapeDtypeStruct((rows, width), jnp.bfloat16),
        scratch_shapes=[
            pltpu.VMEM((rows, depth), jnp.bfloat16),
            pltpu.VMEM((chips, 2, quarters, part, width), jnp.bfloat16),
            pltpu.VMEM((rows, HEAD_SIZE), jnp.float32),
            pltpu.VMEM((rows, HEAD_SIZE), jnp.float32),
            pltpu.VMEM((width // HEAD_SIZE, HEAD_SIZE, rows), jnp.bfloat16),
            pltpu.VMEM((3 * rows, HEAD_SIZE), jnp.bfloat16),
            pltpu.VMEM((3 * rows, HEAD_SIZE), jnp.bfloat16),
            pltpu.VMEM((HEAD_SIZE, 3 * rows), jnp.bfloat16),
            pltpu.VMEM((rows, width), jnp.float32),
            pltpu.VMEM((HEAD_SIZE, width), jnp.float32),
            pltpu.SemaphoreType.DMA((4 * (2 * quarters + 1) + 8,)),
        ],
        compiler_params=pltpu.CompilerParams(vmem_limit_bytes=60 * 1024 * 1024),
        cost_estimate=pl.CostEstimate(
            flops=2 * rows * depth * width + 8 * rows * rows * width,
            bytes_accessed=2 * (rows * depth + depth * width),
            transcendentals=0,
        ),
    )(core, first, low, x, cosine, sine, kv2, kv1, kv0, wa, wb)


def normalize(tokens, norm_gain):
    widened = tokens.astype(jnp.float32)
    mean_sq = jnp.mean(widened * widened, axis=-1, keepdims=True)
    return (widened * lax.rsqrt(mean_sq + 1e-05) * norm_gain.astype(jnp.float32)).astype(
        jnp.bfloat16
    )


def gather_column(mine):
    quarter = mine.shape[0] // lax.axis_size("attn")
    own = lax.dynamic_slice_in_dim(mine, lax.axis_index("attn") * quarter, quarter, 0)
    chips = lax.axis_size("rows") // 2
    same_core = [[2 * z + c for z in range(chips)] for c in range(2)]
    return lax.all_gather(own, "rows", axis=0, tiled=False, axis_index_groups=same_core)


def nothing_kernel(*refs):
    del refs


def after(x, *others):
    anywhere = pl.BlockSpec(memory_space=pl.ANY)
    return pl.pallas_call(
        nothing_kernel,
        in_specs=[anywhere] * (1 + len(others)),
        out_specs=anywhere,
        out_shape=jax.ShapeDtypeStruct(x.shape, x.dtype),
        input_output_aliases={0: 0},
        compiler_params=pltpu.CompilerParams(vmem_limit_bytes=1024 * 1024),
        cost_estimate=pl.CostEstimate(flops=0, bytes_accessed=0, transcendentals=0),
    )(x, *others)


def columns_kernel(first, x_ref, out_ref):
    for n in range(out_ref.shape[0]):
        out_ref[n] = x_ref[..., first : first + out_ref.shape[-1]]


def four_copies(x, first, width):
    parts = lax.axis_size("attn")
    whole = pl.BlockSpec(memory_space=pltpu.VMEM)
    out = jax.ShapeDtypeStruct((parts, *x.shape[:-1], width), x.dtype)
    spread = pl.pallas_call(
        functools.partial(columns_kernel, first),
        in_specs=[whole],
        out_specs=whole,
        out_shape=out,
        compiler_params=pltpu.CompilerParams(vmem_limit_bytes=8 * 1024 * 1024),
        cost_estimate=pl.CostEstimate(flops=0, bytes_accessed=3 * out.size, transcendentals=0),
    )(x)
    return spread


def exchange_attn(copies):
    return lax.all_to_all(copies, "attn", 0, 0, tiled=True)


def swap_cores(half):
    return lax.ppermute(half, "rows", [(i, i ^ 1) for i in range(lax.axis_size("rows"))])


def on_device(
    tokens, norm_gain, w_query, key_projection_weight, value_projection_weight, documents
):
    rows = tokens.shape[0]
    me = lax.axis_index("attn")
    split = 2 * HEAD_SIZE
    column = gather_column(
        jnp.concatenate([key_projection_weight, value_projection_weight, w_query], 1)
    )
    normed = normalize(tokens, norm_gain)
    kv_half = exchange_attn(four_copies(column, 0, split))
    copies = four_copies(column, split, w_query.shape[1])
    query_half = exchange_attn(after(copies, normed[:16, :HEAD_SIZE], kv_half))
    cosine, sine = rotary_tables(me * rows + jnp.arange(rows, dtype=jnp.int32))
    doc_ids = documents[0]
    my_docs = lax.dynamic_slice_in_dim(doc_ids, me * rows, rows)
    begin = jnp.sum((doc_ids[None, :] < my_docs[:, None]).astype(jnp.int32), axis=1)
    low = jnp.maximum(begin - (me - 2) * rows, 0).reshape(-1, QUERY_BLOCK)
    first = low[:, 0] // KEY_BLOCK

    core = (lax.axis_index("rows") % 2).astype(jnp.int32).reshape(1)
    kv = project_kv(core, normed, kv_half, swap_cores(kv_half), cosine, sine)
    kv1 = lax.ppermute(kv, "attn", [(0, 1), (1, 2), (2, 3)])
    kv2 = lax.ppermute(kv, "attn", [(0, 2), (1, 3)])
    query_half = after(query_half, kv1, kv2)
    other = swap_cores(query_half)
    return attend(core, first, low, normed, cosine, sine, kv2, kv1, kv, query_half, other)


def solution(mesh):
    placed = (
        P(("rows", "attn"), None),
        P(),
        P("rows", "tp"),
        P("rows", "tp"),
        P("rows", "tp"),
        P("rows", None),
    )
    return jax.shard_map(
        on_device, mesh=mesh, in_specs=placed, out_specs=P(("rows", "attn"), "tp"), check_vma=False
    )
```

```python
import functools
import math

import jax
import jax.numpy as jnp
from jax import lax
from jax.experimental import pallas as pl
from jax.experimental.pallas import tpu as pltpu
from jax.sharding import PartitionSpec as P

HEAD_SIZE = 128
KEY_BLOCK = 512
QUERY_BLOCK = 128


def rotary_tables(positions):
    half_dim = HEAD_SIZE // 2
    frequency = jnp.exp(
        jnp.arange(half_dim, dtype=jnp.float32) * (-2.0 * math.log(500000.0) / HEAD_SIZE)
    )
    angles = positions.astype(jnp.float32)[:, None] * frequency[None, :]
    cosine, sine = jnp.cos(angles), jnp.sin(angles)
    return jnp.concatenate([cosine, cosine], 1), jnp.concatenate([-sine, sine], 1)


def rotate(u, cosine, sine):
    return u * cosine + pltpu.roll(u, HEAD_SIZE // 2, 1) * sine


def bring_weights(bring, core, chips, own, other, w):
    for k in range(own.shape[0]):
        bring(own.at[k, chips], w.at[chips, core, k])
        bring(other.at[k, chips], w.at[chips, 1 - core, k])


def kv_kernel(
    core_ref, x_ref, wa_ref, wb_ref, cos_ref, sin_ref, out_ref, x, w, cos, sin, sums, sems
):
    rows, depth = x_ref.shape
    width = out_ref.shape[1]
    pieces = 4
    count = wa_ref.shape[1] // pieces
    piece = depth // pieces
    copies = []

    def bring(src, dst):
        copies.append(pltpu.make_async_copy(src, dst, sems.at[len(copies)]))
        copies[-1].start()

    ready = []
    for n in range(pieces):
        begin = len(copies)
        bring_weights(bring, core_ref[0], pl.ds(n * count, count), wa_ref, wb_ref, w)
        take = pl.ds(n * piece, piece)
        bring(x_ref.at[:, take], x.at[:, take])
        ready.append(copies[begin:])
    bring(cos_ref, cos)
    bring(sin_ref, sin)
    for n in range(pieces):
        for copy in ready[n]:
            copy.wait()
        weights = w[n * count : (n + 1) * count].reshape(piece, width)
        part = jnp.dot(
            x[:, n * piece : (n + 1) * piece], weights, preferred_element_type=jnp.float32
        )
        if n == 0:
            sums[...] = part
        else:
            sums[...] += part
    copies[-2].wait()
    copies[-1].wait()
    keys = rotate(sums[:, :HEAD_SIZE], cos[...], sin[...])
    out_ref[:, :HEAD_SIZE] = keys.astype(jnp.bfloat16)
    out_ref[:, HEAD_SIZE:] = sums[:, HEAD_SIZE:].astype(jnp.bfloat16)


def project_kv(core, x, wa, wb, cosine, sine):
    rows, depth = x.shape
    quarters, chips, part, width = wa.shape
    return pl.pallas_call(
        kv_kernel,
        in_specs=[pl.BlockSpec(memory_space=pltpu.SMEM)]
        + [pl.BlockSpec(memory_space=pl.ANY)] * 5,
        out_specs=pl.BlockSpec(memory_space=pltpu.VMEM),
        out_shape=jax.ShapeDtypeStruct((rows, width), jnp.bfloat16),
        scratch_shapes=[
            pltpu.VMEM((rows, depth), jnp.bfloat16),
            pltpu.VMEM((chips, 2, quarters, part, width), jnp.bfloat16),
            pltpu.VMEM((rows, HEAD_SIZE), jnp.float32),
            pltpu.VMEM((rows, HEAD_SIZE), jnp.float32),
            pltpu.VMEM((rows, width), jnp.float32),
            pltpu.SemaphoreType.DMA((4 * (2 * quarters + 1) + 2,)),
        ],
        compiler_params=pltpu.CompilerParams(vmem_limit_bytes=60 * 1024 * 1024),
        cost_estimate=pl.CostEstimate(
            flops=2 * rows * depth * width,
            bytes_accessed=2 * (rows * depth + depth * width + rows * width),
            transcendentals=0,
        ),
    )(core, x, wa, wb, cosine, sine)


def attend_kernel(
    core_ref, first_ref, low_ref, x_ref, cos_ref, sin_ref, kv2_ref, kv1_ref, kv0_ref, wa_ref, wb_ref,
    out_ref, x, w, cos, sin, q, keys, plain, values, sums, acc, sems,
):
    rows, depth = x_ref.shape
    width = out_ref.shape[1]
    heads = width // HEAD_SIZE
    pieces = 4
    quarters, chips = wa_ref.shape[:2]
    count = chips // pieces
    piece = depth // pieces
    copies = []

    def bring(src, dst):
        copies.append(pltpu.make_async_copy(src, dst, sems.at[len(copies)]))
        copies[-1].start()

    ready = []
    for n in range(pieces):
        begin = len(copies)
        some = pl.ds(n * count, count)
        bring_weights(bring, core_ref[0], some, wa_ref, wb_ref, w)
        take = pl.ds(n * piece, piece)
        bring(x_ref.at[:, take], x.at[:, take])
        ready.append(copies[begin:])
        if n == 0:
            begin = len(copies)
            for at, ref in enumerate((kv2_ref, kv1_ref, kv0_ref)):
                part = pl.ds(at * rows, rows)
                bring(ref.at[:, :HEAD_SIZE], keys.at[part])
                bring(ref.at[:, HEAD_SIZE:], plain.at[part])
            bring(cos_ref, cos)
            bring(sin_ref, sin)
            others = copies[begin:]

    for n in range(pieces):
        for copy in ready[n]:
            copy.wait()
        weights = w[n * count : (n + 1) * count].reshape(piece, width)
        part = jnp.dot(
            x[:, n * piece : (n + 1) * piece], weights, preferred_element_type=jnp.float32
        )
        if n == 0:
            sums[...] = part
            for copy in others:
                copy.wait()
            for at in range(0, 3 * rows, rows):
                values[:, at : at + rows] = plain[at : at + rows].T
        else:
            sums[...] += part
    for h in range(heads):
        lanes = slice(h * HEAD_SIZE, (h + 1) * HEAD_SIZE)
        q[h] = rotate(sums[:, lanes], cos[...], sin[...]).T.astype(jnp.bfloat16)

    key_lane = lax.broadcasted_iota(jnp.int32, (KEY_BLOCK, QUERY_BLOCK), 0)
    query_lane = lax.broadcasted_iota(jnp.int32, (KEY_BLOCK, QUERY_BLOCK), 1)
    to_log2 = math.log2(math.e) / math.sqrt(HEAD_SIZE)
    for step in range(rows // QUERY_BLOCK):
        block = slice(step * QUERY_BLOCK, (step + 1) * QUERY_BLOCK)
        queries = jnp.concatenate(
            [q[h, :, block] for h in range(heads)], axis=1
        )
        low = low_ref[step : step + 1, :]
        first_query = 2 * rows + step * QUERY_BLOCK
        acc[...] = jnp.zeros_like(acc)

        def visit(n, carry):
            run_max, run_sum = carry
            start = pl.multiple_of(n * KEY_BLOCK, KEY_BLOCK)
            scores = jnp.dot(
                keys[pl.ds(start, KEY_BLOCK)], queries, preferred_element_type=jnp.float32
            )
            visible = (start + key_lane >= low) & (start + key_lane <= first_query + query_lane)
            visible = jnp.concatenate([visible] * heads, axis=1)
            scores = jnp.where(visible, scores, -1e30)
            new_max = jnp.maximum(run_max, jnp.max(scores, axis=0, keepdims=True))
            factor = jnp.exp2((run_max - new_max) * to_log2)
            weights = jnp.exp2((scores - new_max) * to_log2)
            run_sum = run_sum * factor + jnp.sum(weights, axis=0, keepdims=True)
            acc[...] = acc[...] * factor + jnp.dot(
                values[:, pl.ds(start, KEY_BLOCK)],
                weights.astype(jnp.bfloat16),
                preferred_element_type=jnp.float32,
            )
            return new_max, run_sum

        initial = (
            jnp.full((1, width), -1e30, jnp.float32),
            jnp.zeros((1, width), jnp.float32),
        )
        last = (first_query + QUERY_BLOCK - 1) // KEY_BLOCK + 1
        _, run_sum = lax.fori_loop(first_ref[step], last, visit, initial)
        mixed = acc[...] / run_sum
        for h in range(heads):
            lanes = slice(h * HEAD_SIZE, (h + 1) * HEAD_SIZE)
            out_ref[block, lanes] = mixed[:, lanes].T.astype(jnp.bfloat16)


def attend(core, first, low, x, cosine, sine, kv2, kv1, kv0, wa, wb):
    rows, depth = x.shape
    quarters, chips, part, width = wa.shape
    whole = pl.BlockSpec(memory_space=pltpu.VMEM)
    return pl.pallas_call(
        attend_kernel,
        in_specs=[pl.BlockSpec(memory_space=pltpu.SMEM)] * 2
        + [whole]
        + [pl.BlockSpec(memory_space=pl.ANY)] * 8,
        out_specs=whole,
        out_shape=jax.ShapeDtypeStruct((rows, width), jnp.bfloat16),
        scratch_shapes=[
            pltpu.VMEM((rows, depth), jnp.bfloat16),
            pltpu.VMEM((chips, 2, quarters, part, width), jnp.bfloat16),
            pltpu.VMEM((rows, HEAD_SIZE), jnp.float32),
            pltpu.VMEM((rows, HEAD_SIZE), jnp.float32),
            pltpu.VMEM((width // HEAD_SIZE, HEAD_SIZE, rows), jnp.bfloat16),
            pltpu.VMEM((3 * rows, HEAD_SIZE), jnp.bfloat16),
            pltpu.VMEM((3 * rows, HEAD_SIZE), jnp.bfloat16),
            pltpu.VMEM((HEAD_SIZE, 3 * rows), jnp.bfloat16),
            pltpu.VMEM((rows, width), jnp.float32),
            pltpu.VMEM((HEAD_SIZE, width), jnp.float32),
            pltpu.SemaphoreType.DMA((4 * (2 * quarters + 1) + 8,)),
        ],
        compiler_params=pltpu.CompilerParams(vmem_limit_bytes=60 * 1024 * 1024),
        cost_estimate=pl.CostEstimate(
            flops=2 * rows * depth * width + 8 * rows * rows * width,
            bytes_accessed=2 * (rows * depth + depth * width),
            transcendentals=0,
        ),
    )(core, first, low, x, cosine, sine, kv2, kv1, kv0, wa, wb)


def normalize(tokens, norm_gain):
    widened = tokens.astype(jnp.float32)
    mean_sq = jnp.mean(widened * widened, axis=-1, keepdims=True)
    return (widened * lax.rsqrt(mean_sq + 1e-05) * norm_gain.astype(jnp.float32)).astype(
        jnp.bfloat16
    )


def gather_column(mine):
    quarter = mine.shape[0] // lax.axis_size("attn")
    own = lax.dynamic_slice_in_dim(mine, lax.axis_index("attn") * quarter, quarter, 0)
    chips = lax.axis_size("rows") // 2
    same_core = [[2 * z + c for z in range(chips)] for c in range(2)]
    return lax.all_gather(own, "rows", axis=0, tiled=False, axis_index_groups=same_core)


def nothing_kernel(*refs):
    del refs


def after(x, *others):
    anywhere = pl.BlockSpec(memory_space=pl.ANY)
    return pl.pallas_call(
        nothing_kernel,
        in_specs=[anywhere] * (1 + len(others)),
        out_specs=anywhere,
        out_shape=jax.ShapeDtypeStruct(x.shape, x.dtype),
        input_output_aliases={0: 0},
        compiler_params=pltpu.CompilerParams(vmem_limit_bytes=1024 * 1024),
        cost_estimate=pl.CostEstimate(flops=0, bytes_accessed=0, transcendentals=0),
    )(x, *others)


def columns_kernel(first, x_ref, out_ref):
    for n in range(out_ref.shape[0]):
        out_ref[n] = x_ref[..., first : first + out_ref.shape[-1]]


def four_copies(x, first, width):
    parts = lax.axis_size("attn")
    whole = pl.BlockSpec(memory_space=pltpu.VMEM)
    out = jax.ShapeDtypeStruct((parts, *x.shape[:-1], width), x.dtype)
    spread = pl.pallas_call(
        functools.partial(columns_kernel, first),
        in_specs=[whole],
        out_specs=whole,
        out_shape=out,
        compiler_params=pltpu.CompilerParams(vmem_limit_bytes=8 * 1024 * 1024),
        cost_estimate=pl.CostEstimate(flops=0, bytes_accessed=3 * out.size, transcendentals=0),
    )(x)
    return spread


def exchange_attn(copies):
    return lax.all_to_all(copies, "attn", 0, 0, tiled=True)


def swap_cores(half):
    return lax.ppermute(half, "rows", [(i, i ^ 1) for i in range(lax.axis_size("rows"))])


def on_device(
    tokens, norm_gain, w_query, key_projection_weight, value_projection_weight, documents
):
    rows = tokens.shape[0]
    me = lax.axis_index("attn")
    split = 2 * HEAD_SIZE
    column = gather_column(
        jnp.concatenate([key_projection_weight, value_projection_weight, w_query], 1)
    )
    normed = normalize(tokens, norm_gain)
    kv_half = exchange_attn(four_copies(column, 0, split))
    copies = four_copies(column, split, w_query.shape[1])
    query_half = exchange_attn(after(copies, normed[:16, :HEAD_SIZE], kv_half))
    cosine, sine = rotary_tables(me * rows + jnp.arange(rows, dtype=jnp.int32))
    doc_ids = documents[0]
    my_docs = lax.dynamic_slice_in_dim(doc_ids, me * rows, rows)
    begin = jnp.sum((doc_ids[None, :] < my_docs[:, None]).astype(jnp.int32), axis=1)
    low = jnp.maximum(begin - (me - 2) * rows, 0).reshape(-1, QUERY_BLOCK)
    first = low[:, 0] // KEY_BLOCK

    core = (lax.axis_index("rows") % 2).astype(jnp.int32).reshape(1)
    kv = project_kv(core, normed, kv_half, swap_cores(kv_half), cosine, sine)
    kv1 = lax.ppermute(kv, "attn", [(0, 1), (1, 2), (2, 3)])
    kv2 = lax.ppermute(kv, "attn", [(0, 2), (1, 3)])
    query_half = after(query_half, kv1, kv2)
    other = swap_cores(query_half)
    return attend(core, first, low, normed, cosine, sine, kv2, kv1, kv, query_half, other)


def solution(mesh):
    placed = (
        P(("rows", "attn"), None),
        P(),
        P("rows", "tp"),
        P("rows", "tp"),
        P("rows", "tp"),
        P("rows", None),
    )
    return jax.shard_map(
        on_device, mesh=mesh, in_specs=placed, out_specs=P(("rows", "attn"), "tp"), check_vma=False
    )
```

```python
import functools
import math

import jax
import jax.numpy as jnp
from jax import lax
from jax.experimental import pallas as pl
from jax.experimental.pallas import tpu as pltpu
from jax.sharding import PartitionSpec as P

HEAD_SIZE = 128
KEY_BLOCK = 512
QUERY_BLOCK = 128


def rotary_tables(positions):
    half_dim = HEAD_SIZE // 2
    frequency = jnp.exp(
        jnp.arange(half_dim, dtype=jnp.float32) * (-2.0 * math.log(500000.0) / HEAD_SIZE)
    )
    angles = positions.astype(jnp.float32)[:, None] * frequency[None, :]
    cosine, sine = jnp.cos(angles), jnp.sin(angles)
    return jnp.concatenate([cosine, cosine], 1), jnp.concatenate([-sine, sine], 1)


def rotate(u, cosine, sine):
    return u * cosine + pltpu.roll(u, HEAD_SIZE // 2, 1) * sine


def bring_weights(bring, core, chips, own, other, w):
    for k in range(own.shape[0]):
        bring(own.at[k, chips], w.at[chips, core, k])
        bring(other.at[k, chips], w.at[chips, 1 - core, k])


def kv_kernel(
    core_ref, x_ref, wa_ref, wb_ref, cos_ref, sin_ref, out_ref, x, w, cos, sin, sums, sems
):
    rows, depth = x_ref.shape
    width = out_ref.shape[1]
    pieces = 4
    count = wa_ref.shape[1] // pieces
    piece = depth // pieces
    copies = []

    def bring(src, dst):
        copies.append(pltpu.make_async_copy(src, dst, sems.at[len(copies)]))
        copies[-1].start()

    ready = []
    for n in range(pieces):
        begin = len(copies)
        bring_weights(bring, core_ref[0], pl.ds(n * count, count), wa_ref, wb_ref, w)
        take = pl.ds(n * piece, piece)
        bring(x_ref.at[:, take], x.at[:, take])
        ready.append(copies[begin:])
    bring(cos_ref, cos)
    bring(sin_ref, sin)
    for n in range(pieces):
        for copy in ready[n]:
            copy.wait()
        weights = w[n * count : (n + 1) * count].reshape(piece, width)
        part = jnp.dot(
            x[:, n * piece : (n + 1) * piece], weights, preferred_element_type=jnp.float32
        )
        if n == 0:
            sums[...] = part
        else:
            sums[...] += part
    copies[-2].wait()
    copies[-1].wait()
    keys = rotate(sums[:, :HEAD_SIZE], cos[...], sin[...])
    out_ref[:, :HEAD_SIZE] = keys.astype(jnp.bfloat16)
    out_ref[:, HEAD_SIZE:] = sums[:, HEAD_SIZE:].astype(jnp.bfloat16)


def project_kv(core, x, wa, wb, cosine, sine):
    rows, depth = x.shape
    quarters, chips, part, width = wa.shape
    return pl.pallas_call(
        kv_kernel,
        in_specs=[pl.BlockSpec(memory_space=pltpu.SMEM)]
        + [pl.BlockSpec(memory_space=pl.ANY)] * 5,
        out_specs=pl.BlockSpec(memory_space=pltpu.VMEM),
        out_shape=jax.ShapeDtypeStruct((rows, width), jnp.bfloat16),
        scratch_shapes=[
            pltpu.VMEM((rows, depth), jnp.bfloat16),
            pltpu.VMEM((chips, 2, quarters, part, width), jnp.bfloat16),
            pltpu.VMEM((rows, HEAD_SIZE), jnp.float32),
            pltpu.VMEM((rows, HEAD_SIZE), jnp.float32),
            pltpu.VMEM((rows, width), jnp.float32),
            pltpu.SemaphoreType.DMA((4 * (2 * quarters + 1) + 2,)),
        ],
        compiler_params=pltpu.CompilerParams(vmem_limit_bytes=60 * 1024 * 1024),
        cost_estimate=pl.CostEstimate(
            flops=2 * rows * depth * width,
            bytes_accessed=2 * (rows * depth + depth * width + rows * width),
            transcendentals=0,
        ),
    )(core, x, wa, wb, cosine, sine)


def attend_kernel(
    core_ref, first_ref, low_ref, x_ref, cos_ref, sin_ref, kv2_ref, kv1_ref, kv0_ref, wa_ref, wb_ref,
    out_ref, x, w, cos, sin, q, keys, plain, values, sums, acc, sems,
):
    rows, depth = x_ref.shape
    width = out_ref.shape[1]
    heads = width // HEAD_SIZE
    pieces = 4
    quarters, chips = wa_ref.shape[:2]
    count = chips // pieces
    piece = depth // pieces
    copies = []

    def bring(src, dst):
        copies.append(pltpu.make_async_copy(src, dst, sems.at[len(copies)]))
        copies[-1].start()

    ready = []
    for n in range(pieces):
        begin = len(copies)
        some = pl.ds(n * count, count)
        bring_weights(bring, core_ref[0], some, wa_ref, wb_ref, w)
        take = pl.ds(n * piece, piece)
        bring(x_ref.at[:, take], x.at[:, take])
        ready.append(copies[begin:])
        if n == 0:
            begin = len(copies)
            for at, ref in enumerate((kv2_ref, kv1_ref, kv0_ref)):
                part = pl.ds(at * rows, rows)
                bring(ref.at[:, :HEAD_SIZE], keys.at[part])
                bring(ref.at[:, HEAD_SIZE:], plain.at[part])
            bring(cos_ref, cos)
            bring(sin_ref, sin)
            others = copies[begin:]

    for n in range(pieces):
        for copy in ready[n]:
            copy.wait()
        weights = w[n * count : (n + 1) * count].reshape(piece, width)
        part = jnp.dot(
            x[:, n * piece : (n + 1) * piece], weights, preferred_element_type=jnp.float32
        )
        if n == 0:
            sums[...] = part
            for copy in others:
                copy.wait()
            for at in range(0, 3 * rows, rows):
                values[:, at : at + rows] = plain[at : at + rows].T
        else:
            sums[...] += part
    for h in range(heads):
        lanes = slice(h * HEAD_SIZE, (h + 1) * HEAD_SIZE)
        q[h] = rotate(sums[:, lanes], cos[...], sin[...]).T.astype(jnp.bfloat16)

    to_log2 = math.log2(math.e) / math.sqrt(HEAD_SIZE)
    for step in range(rows // QUERY_BLOCK):
        block = slice(step * QUERY_BLOCK, (step + 1) * QUERY_BLOCK)
        queries = jnp.concatenate(
            [q[h, :, block] for h in range(heads)], axis=1
        )
        low = low_ref[step : step + 1, :]
        first_query = 2 * rows + step * QUERY_BLOCK
        acc[...] = jnp.zeros_like(acc)

        def visit(start, size, carry):
            run_max, run_sum = carry
            scores = jnp.dot(
                keys[pl.ds(start, size)], queries, preferred_element_type=jnp.float32
            )
            key_at = start + lax.broadcasted_iota(jnp.int32, (size, QUERY_BLOCK), 0)
            query_at = first_query + lax.broadcasted_iota(jnp.int32, (size, QUERY_BLOCK), 1)
            visible = (key_at >= low) & (key_at <= query_at)
            visible = jnp.concatenate([visible] * heads, axis=1)
            scores = jnp.where(visible, scores, -1e30)
            new_max = jnp.maximum(run_max, jnp.max(scores, axis=0, keepdims=True))
            factor = jnp.exp2((run_max - new_max) * to_log2)
            weights = jnp.exp2((scores - new_max) * to_log2)
            run_sum = run_sum * factor + jnp.sum(weights, axis=0, keepdims=True)
            acc[...] = acc[...] * factor + jnp.dot(
                values[:, pl.ds(start, size)],
                weights.astype(jnp.bfloat16),
                preferred_element_type=jnp.float32,
            )
            return new_max, run_sum

        def visit_earlier(n, carry):
            return visit(pl.multiple_of(n * KEY_BLOCK, KEY_BLOCK), KEY_BLOCK, carry)

        initial = (
            jnp.full((1, width), -1e30, jnp.float32),
            jnp.zeros((1, width), jnp.float32),
        )
        carry = lax.fori_loop(first_ref[step], 2 * rows // KEY_BLOCK, visit_earlier, initial)
        _, run_sum = visit(2 * rows, (step + 1) * QUERY_BLOCK, carry)
        mixed = acc[...] / run_sum
        for h in range(heads):
            lanes = slice(h * HEAD_SIZE, (h + 1) * HEAD_SIZE)
            out_ref[block, lanes] = mixed[:, lanes].T.astype(jnp.bfloat16)


def attend(core, first, low, x, cosine, sine, kv2, kv1, kv0, wa, wb):
    rows, depth = x.shape
    quarters, chips, part, width = wa.shape
    whole = pl.BlockSpec(memory_space=pltpu.VMEM)
    return pl.pallas_call(
        attend_kernel,
        in_specs=[pl.BlockSpec(memory_space=pltpu.SMEM)] * 2
        + [whole]
        + [pl.BlockSpec(memory_space=pl.ANY)] * 8,
        out_specs=whole,
        out_shape=jax.ShapeDtypeStruct((rows, width), jnp.bfloat16),
        scratch_shapes=[
            pltpu.VMEM((rows, depth), jnp.bfloat16),
            pltpu.VMEM((chips, 2, quarters, part, width), jnp.bfloat16),
            pltpu.VMEM((rows, HEAD_SIZE), jnp.float32),
            pltpu.VMEM((rows, HEAD_SIZE), jnp.float32),
            pltpu.VMEM((width // HEAD_SIZE, HEAD_SIZE, rows), jnp.bfloat16),
            pltpu.VMEM((3 * rows, HEAD_SIZE), jnp.bfloat16),
            pltpu.VMEM((3 * rows, HEAD_SIZE), jnp.bfloat16),
            pltpu.VMEM((HEAD_SIZE, 3 * rows), jnp.bfloat16),
            pltpu.VMEM((rows, width), jnp.float32),
            pltpu.VMEM((HEAD_SIZE, width), jnp.float32),
            pltpu.SemaphoreType.DMA((4 * (2 * quarters + 1) + 8,)),
        ],
        compiler_params=pltpu.CompilerParams(vmem_limit_bytes=60 * 1024 * 1024),
        cost_estimate=pl.CostEstimate(
            flops=2 * rows * depth * width + 8 * rows * rows * width,
            bytes_accessed=2 * (rows * depth + depth * width),
            transcendentals=0,
        ),
    )(core, first, low, x, cosine, sine, kv2, kv1, kv0, wa, wb)


def normalize(tokens, norm_gain):
    widened = tokens.astype(jnp.float32)
    mean_sq = jnp.mean(widened * widened, axis=-1, keepdims=True)
    return (widened * lax.rsqrt(mean_sq + 1e-05) * norm_gain.astype(jnp.float32)).astype(
        jnp.bfloat16
    )


def gather_column(mine):
    quarter = mine.shape[0] // lax.axis_size("attn")
    own = lax.dynamic_slice_in_dim(mine, lax.axis_index("attn") * quarter, quarter, 0)
    chips = lax.axis_size("rows") // 2
    same_core = [[2 * z + c for z in range(chips)] for c in range(2)]
    return lax.all_gather(own, "rows", axis=0, tiled=False, axis_index_groups=same_core)


def nothing_kernel(*refs):
    del refs


def after(x, *others):
    anywhere = pl.BlockSpec(memory_space=pl.ANY)
    return pl.pallas_call(
        nothing_kernel,
        in_specs=[anywhere] * (1 + len(others)),
        out_specs=anywhere,
        out_shape=jax.ShapeDtypeStruct(x.shape, x.dtype),
        input_output_aliases={0: 0},
        compiler_params=pltpu.CompilerParams(vmem_limit_bytes=1024 * 1024),
        cost_estimate=pl.CostEstimate(flops=0, bytes_accessed=0, transcendentals=0),
    )(x, *others)


def columns_kernel(first, x_ref, out_ref):
    for n in range(out_ref.shape[0]):
        out_ref[n] = x_ref[..., first : first + out_ref.shape[-1]]


def four_copies(x, first, width):
    parts = lax.axis_size("attn")
    whole = pl.BlockSpec(memory_space=pltpu.VMEM)
    out = jax.ShapeDtypeStruct((parts, *x.shape[:-1], width), x.dtype)
    spread = pl.pallas_call(
        functools.partial(columns_kernel, first),
        in_specs=[whole],
        out_specs=whole,
        out_shape=out,
        compiler_params=pltpu.CompilerParams(vmem_limit_bytes=8 * 1024 * 1024),
        cost_estimate=pl.CostEstimate(flops=0, bytes_accessed=3 * out.size, transcendentals=0),
    )(x)
    return spread


def exchange_attn(copies):
    return lax.all_to_all(copies, "attn", 0, 0, tiled=True)


def swap_cores(half):
    return lax.ppermute(half, "rows", [(i, i ^ 1) for i in range(lax.axis_size("rows"))])


def on_device(
    tokens, norm_gain, w_query, key_projection_weight, value_projection_weight, documents
):
    rows = tokens.shape[0]
    me = lax.axis_index("attn")
    split = 2 * HEAD_SIZE
    column = gather_column(
        jnp.concatenate([key_projection_weight, value_projection_weight, w_query], 1)
    )
    normed = normalize(tokens, norm_gain)
    kv_half = exchange_attn(four_copies(column, 0, split))
    copies = four_copies(column, split, w_query.shape[1])
    query_half = exchange_attn(after(copies, normed[:16, :HEAD_SIZE], kv_half))
    cosine, sine = rotary_tables(me * rows + jnp.arange(rows, dtype=jnp.int32))
    doc_ids = documents[0]
    my_docs = lax.dynamic_slice_in_dim(doc_ids, me * rows, rows)
    begin = jnp.sum((doc_ids[None, :] < my_docs[:, None]).astype(jnp.int32), axis=1)
    low = jnp.maximum(begin - (me - 2) * rows, 0).reshape(-1, QUERY_BLOCK)
    first = low[:, 0] // KEY_BLOCK

    core = (lax.axis_index("rows") % 2).astype(jnp.int32).reshape(1)
    kv = project_kv(core, normed, kv_half, swap_cores(kv_half), cosine, sine)
    kv1 = lax.ppermute(kv, "attn", [(0, 1), (1, 2), (2, 3)])
    kv2 = lax.ppermute(kv, "attn", [(0, 2), (1, 3)])
    query_half = after(query_half, kv1, kv2)
    other = swap_cores(query_half)
    return attend(core, first, low, normed, cosine, sine, kv2, kv1, kv, query_half, other)


def solution(mesh):
    placed = (
        P(("rows", "attn"), None),
        P(),
        P("rows", "tp"),
        P("rows", "tp"),
        P("rows", "tp"),
        P("rows", None),
    )
    return jax.shard_map(
        on_device, mesh=mesh, in_specs=placed, out_specs=P(("rows", "attn"), "tp"), check_vma=False
    )
```

```python
import functools
import math

import jax
import jax.numpy as jnp
from jax import lax
from jax.experimental import pallas as pl
from jax.experimental.pallas import tpu as pltpu
from jax.sharding import PartitionSpec as P

HEAD_SIZE = 128
KEY_BLOCK = 512
QUERY_BLOCK = 128


def rotary_tables(positions):
    half_dim = HEAD_SIZE // 2
    frequency = jnp.exp(
        jnp.arange(half_dim, dtype=jnp.float32) * (-2.0 * math.log(500000.0) / HEAD_SIZE)
    )
    angles = positions.astype(jnp.float32)[:, None] * frequency[None, :]
    cosine, sine = jnp.cos(angles), jnp.sin(angles)
    return jnp.concatenate([cosine, cosine], 1), jnp.concatenate([-sine, sine], 1)


def rotate(u, cosine, sine):
    return u * cosine + pltpu.roll(u, HEAD_SIZE // 2, 1) * sine


def bring_weights(bring, core, chips, own, other, w):
    for k in range(own.shape[0]):
        bring(own.at[k, chips], w.at[chips, core, k])
        bring(other.at[k, chips], w.at[chips, 1 - core, k])


def kv_kernel(
    core_ref, x_ref, wa_ref, wb_ref, cos_ref, sin_ref, out_ref, x, w, cos, sin, sums, sems
):
    rows, depth = x_ref.shape
    width = out_ref.shape[1]
    pieces = 4
    count = wa_ref.shape[1] // pieces
    piece = depth // pieces
    copies = []

    def bring(src, dst):
        copies.append(pltpu.make_async_copy(src, dst, sems.at[len(copies)]))
        copies[-1].start()

    ready = []
    for n in range(pieces):
        begin = len(copies)
        bring_weights(bring, core_ref[0], pl.ds(n * count, count), wa_ref, wb_ref, w)
        take = pl.ds(n * piece, piece)
        bring(x_ref.at[:, take], x.at[:, take])
        ready.append(copies[begin:])
    bring(cos_ref, cos)
    bring(sin_ref, sin)
    for n in range(pieces):
        for copy in ready[n]:
            copy.wait()
        weights = w[n * count : (n + 1) * count].reshape(piece, width)
        part = jnp.dot(
            x[:, n * piece : (n + 1) * piece], weights, preferred_element_type=jnp.float32
        )
        if n == 0:
            sums[...] = part
        else:
            sums[...] += part
    copies[-2].wait()
    copies[-1].wait()
    keys = rotate(sums[:, :HEAD_SIZE], cos[...], sin[...])
    out_ref[:, :HEAD_SIZE] = keys.astype(jnp.bfloat16)
    out_ref[:, HEAD_SIZE:] = sums[:, HEAD_SIZE:].astype(jnp.bfloat16)


def project_kv(core, x, wa, wb, cosine, sine):
    rows, depth = x.shape
    quarters, chips, part, width = wa.shape
    return pl.pallas_call(
        kv_kernel,
        in_specs=[pl.BlockSpec(memory_space=pltpu.SMEM)]
        + [pl.BlockSpec(memory_space=pl.ANY)] * 5,
        out_specs=pl.BlockSpec(memory_space=pltpu.VMEM),
        out_shape=jax.ShapeDtypeStruct((rows, width), jnp.bfloat16),
        scratch_shapes=[
            pltpu.VMEM((rows, depth), jnp.bfloat16),
            pltpu.VMEM((chips, 2, quarters, part, width), jnp.bfloat16),
            pltpu.VMEM((rows, HEAD_SIZE), jnp.float32),
            pltpu.VMEM((rows, HEAD_SIZE), jnp.float32),
            pltpu.VMEM((rows, width), jnp.float32),
            pltpu.SemaphoreType.DMA((4 * (2 * quarters + 1) + 2,)),
        ],
        compiler_params=pltpu.CompilerParams(vmem_limit_bytes=60 * 1024 * 1024),
        cost_estimate=pl.CostEstimate(
            flops=2 * rows * depth * width,
            bytes_accessed=2 * (rows * depth + depth * width + rows * width),
            transcendentals=0,
        ),
    )(core, x, wa, wb, cosine, sine)


def attend_kernel(
    core_ref, first_ref, low_ref, x_ref, cos_ref, sin_ref, kv2_ref, kv1_ref, kv0_ref, wa_ref, wb_ref,
    out_ref, x, w, cos, sin, q, keys, plain, values, sums, acc, sems,
):
    rows, depth = x_ref.shape
    width = out_ref.shape[1]
    heads = width // HEAD_SIZE
    pieces = 4
    quarters, chips = wa_ref.shape[:2]
    count = chips // pieces
    piece = depth // pieces
    copies = []

    def bring(src, dst):
        copies.append(pltpu.make_async_copy(src, dst, sems.at[len(copies)]))
        copies[-1].start()

    ready = []
    for n in range(pieces):
        begin = len(copies)
        some = pl.ds(n * count, count)
        bring_weights(bring, core_ref[0], some, wa_ref, wb_ref, w)
        take = pl.ds(n * piece, piece)
        bring(x_ref.at[:, take], x.at[:, take])
        ready.append(copies[begin:])
        if n == 0:
            begin = len(copies)
            for at, ref in enumerate((kv2_ref, kv1_ref, kv0_ref)):
                part = pl.ds(at * rows, rows)
                bring(ref.at[:, :HEAD_SIZE], keys.at[part])
                bring(ref.at[:, HEAD_SIZE:], plain.at[part])
            bring(cos_ref, cos)
            bring(sin_ref, sin)
            others = copies[begin:]

    for n in range(pieces):
        for copy in ready[n]:
            copy.wait()
        weights = w[n * count : (n + 1) * count].reshape(piece, width)
        part = jnp.dot(
            x[:, n * piece : (n + 1) * piece], weights, preferred_element_type=jnp.float32
        )
        if n == 0:
            sums[...] = part
            for copy in others:
                copy.wait()
            for at in range(0, 3 * rows, rows):
                values[:, at : at + rows] = plain[at : at + rows].T
        else:
            sums[...] += part
    for h in range(heads):
        lanes = slice(h * HEAD_SIZE, (h + 1) * HEAD_SIZE)
        q[h] = rotate(sums[:, lanes], cos[...], sin[...]).T.astype(jnp.bfloat16)

    to_log2 = math.log2(math.e) / math.sqrt(HEAD_SIZE)
    for step in range(rows // QUERY_BLOCK):
        block = slice(step * QUERY_BLOCK, (step + 1) * QUERY_BLOCK)
        queries = jnp.concatenate(
            [q[h, :, block] for h in range(heads)], axis=1
        )
        low = low_ref[step : step + 1, :]
        first_query = 2 * rows + step * QUERY_BLOCK
        acc[...] = jnp.zeros_like(acc)

        def visit(start, size, carry):
            run_max, run_sum = carry
            scores = jnp.dot(
                keys[pl.ds(start, size)], queries, preferred_element_type=jnp.float32
            )
            key_at = start + lax.broadcasted_iota(jnp.int32, (size, QUERY_BLOCK), 0)
            query_at = first_query + lax.broadcasted_iota(jnp.int32, (size, QUERY_BLOCK), 1)
            visible = (key_at >= low) & (key_at <= query_at)
            visible = jnp.concatenate([visible] * heads, axis=1)
            scores = jnp.where(visible, scores, -1e30)
            new_max = jnp.maximum(run_max, jnp.max(scores, axis=0, keepdims=True))
            factor = jnp.exp2((run_max - new_max) * to_log2)
            weights = jnp.exp2((scores - new_max) * to_log2)
            run_sum = run_sum * factor + jnp.sum(weights, axis=0, keepdims=True)
            acc[...] = acc[...] * factor + jnp.dot(
                values[:, pl.ds(start, size)],
                weights.astype(jnp.bfloat16),
                preferred_element_type=jnp.float32,
            )
            return new_max, run_sum

        def visit_earlier(n, carry):
            return visit(pl.multiple_of(n * KEY_BLOCK, KEY_BLOCK), KEY_BLOCK, carry)

        initial = (
            jnp.full((1, width), -1e30, jnp.float32),
            jnp.zeros((1, width), jnp.float32),
        )
        half = KEY_BLOCK // 2
        first = jnp.minimum(first_ref[step], 2 * rows // half)

        def visit_half(n, carry):
            return visit(pl.multiple_of((first + n) * half, half), half, carry)

        carry = lax.fori_loop(0, first % 2, visit_half, initial)
        carry = lax.fori_loop((first + 1) // 2, 2 * rows // KEY_BLOCK, visit_earlier, carry)
        _, run_sum = visit(2 * rows, (step + 1) * QUERY_BLOCK, carry)
        mixed = acc[...] / run_sum
        for h in range(heads):
            lanes = slice(h * HEAD_SIZE, (h + 1) * HEAD_SIZE)
            out_ref[block, lanes] = mixed[:, lanes].T.astype(jnp.bfloat16)


def attend(core, first, low, x, cosine, sine, kv2, kv1, kv0, wa, wb):
    rows, depth = x.shape
    quarters, chips, part, width = wa.shape
    whole = pl.BlockSpec(memory_space=pltpu.VMEM)
    return pl.pallas_call(
        attend_kernel,
        in_specs=[pl.BlockSpec(memory_space=pltpu.SMEM)] * 2
        + [whole]
        + [pl.BlockSpec(memory_space=pl.ANY)] * 8,
        out_specs=whole,
        out_shape=jax.ShapeDtypeStruct((rows, width), jnp.bfloat16),
        scratch_shapes=[
            pltpu.VMEM((rows, depth), jnp.bfloat16),
            pltpu.VMEM((chips, 2, quarters, part, width), jnp.bfloat16),
            pltpu.VMEM((rows, HEAD_SIZE), jnp.float32),
            pltpu.VMEM((rows, HEAD_SIZE), jnp.float32),
            pltpu.VMEM((width // HEAD_SIZE, HEAD_SIZE, rows), jnp.bfloat16),
            pltpu.VMEM((3 * rows, HEAD_SIZE), jnp.bfloat16),
            pltpu.VMEM((3 * rows, HEAD_SIZE), jnp.bfloat16),
            pltpu.VMEM((HEAD_SIZE, 3 * rows), jnp.bfloat16),
            pltpu.VMEM((rows, width), jnp.float32),
            pltpu.VMEM((HEAD_SIZE, width), jnp.float32),
            pltpu.SemaphoreType.DMA((4 * (2 * quarters + 1) + 8,)),
        ],
        compiler_params=pltpu.CompilerParams(vmem_limit_bytes=60 * 1024 * 1024),
        cost_estimate=pl.CostEstimate(
            flops=2 * rows * depth * width + 8 * rows * rows * width,
            bytes_accessed=2 * (rows * depth + depth * width),
            transcendentals=0,
        ),
    )(core, first, low, x, cosine, sine, kv2, kv1, kv0, wa, wb)


def normalize(tokens, norm_gain):
    widened = tokens.astype(jnp.float32)
    mean_sq = jnp.mean(widened * widened, axis=-1, keepdims=True)
    return (widened * lax.rsqrt(mean_sq + 1e-05) * norm_gain.astype(jnp.float32)).astype(
        jnp.bfloat16
    )


def gather_column(mine):
    quarter = mine.shape[0] // lax.axis_size("attn")
    own = lax.dynamic_slice_in_dim(mine, lax.axis_index("attn") * quarter, quarter, 0)
    chips = lax.axis_size("rows") // 2
    same_core = [[2 * z + c for z in range(chips)] for c in range(2)]
    return lax.all_gather(own, "rows", axis=0, tiled=False, axis_index_groups=same_core)


def nothing_kernel(*refs):
    del refs


def after(x, *others):
    anywhere = pl.BlockSpec(memory_space=pl.ANY)
    return pl.pallas_call(
        nothing_kernel,
        in_specs=[anywhere] * (1 + len(others)),
        out_specs=anywhere,
        out_shape=jax.ShapeDtypeStruct(x.shape, x.dtype),
        input_output_aliases={0: 0},
        compiler_params=pltpu.CompilerParams(vmem_limit_bytes=1024 * 1024),
        cost_estimate=pl.CostEstimate(flops=0, bytes_accessed=0, transcendentals=0),
    )(x, *others)


def columns_kernel(first, x_ref, out_ref):
    for n in range(out_ref.shape[0]):
        out_ref[n] = x_ref[..., first : first + out_ref.shape[-1]]


def four_copies(x, first, width):
    parts = lax.axis_size("attn")
    whole = pl.BlockSpec(memory_space=pltpu.VMEM)
    out = jax.ShapeDtypeStruct((parts, *x.shape[:-1], width), x.dtype)
    spread = pl.pallas_call(
        functools.partial(columns_kernel, first),
        in_specs=[whole],
        out_specs=whole,
        out_shape=out,
        compiler_params=pltpu.CompilerParams(vmem_limit_bytes=8 * 1024 * 1024),
        cost_estimate=pl.CostEstimate(flops=0, bytes_accessed=3 * out.size, transcendentals=0),
    )(x)
    return spread


def exchange_attn(copies):
    return lax.all_to_all(copies, "attn", 0, 0, tiled=True)


def swap_cores(half):
    return lax.ppermute(half, "rows", [(i, i ^ 1) for i in range(lax.axis_size("rows"))])


def on_device(
    tokens, norm_gain, w_query, key_projection_weight, value_projection_weight, documents
):
    rows = tokens.shape[0]
    me = lax.axis_index("attn")
    split = 2 * HEAD_SIZE
    column = gather_column(
        jnp.concatenate([key_projection_weight, value_projection_weight, w_query], 1)
    )
    normed = normalize(tokens, norm_gain)
    kv_half = exchange_attn(four_copies(column, 0, split))
    copies = four_copies(column, split, w_query.shape[1])
    query_half = exchange_attn(after(copies, normed[:16, :HEAD_SIZE], kv_half))
    cosine, sine = rotary_tables(me * rows + jnp.arange(rows, dtype=jnp.int32))
    doc_ids = documents[0]
    my_docs = lax.dynamic_slice_in_dim(doc_ids, me * rows, rows)
    begin = jnp.sum((doc_ids[None, :] < my_docs[:, None]).astype(jnp.int32), axis=1)
    low = jnp.maximum(begin - (me - 2) * rows, 0).reshape(-1, QUERY_BLOCK)
    first = low[:, 0] // (KEY_BLOCK // 2)

    core = (lax.axis_index("rows") % 2).astype(jnp.int32).reshape(1)
    kv = project_kv(core, normed, kv_half, swap_cores(kv_half), cosine, sine)
    kv1 = lax.ppermute(kv, "attn", [(0, 1), (1, 2), (2, 3)])
    kv2 = lax.ppermute(kv, "attn", [(0, 2), (1, 3)])
    query_half = after(query_half, kv1, kv2)
    other = swap_cores(query_half)
    return attend(core, first, low, normed, cosine, sine, kv2, kv1, kv, query_half, other)


def solution(mesh):
    placed = (
        P(("rows", "attn"), None),
        P(),
        P("rows", "tp"),
        P("rows", "tp"),
        P("rows", "tp"),
        P("rows", None),
    )
    return jax.shard_map(
        on_device, mesh=mesh, in_specs=placed, out_specs=P(("rows", "attn"), "tp"), check_vma=False
    )
```
